128 devices in a mesh: grp: 4 (over z_hi, core), wide: 32 (over y, z_lo, x).
Axes of the slice: x: 4, y: 4, z: 4 (z_hi: 2, z_lo: 2; z = z_hi * 2 + z_lo), core: 2. Of those that a mesh axis runs over, the one named last changes fastest.
Arguments:
- queries: bfloat16 [256, 32, 128], P(('grp', 'wide')), may hold values from -6 to 6
- centroids: bfloat16 [131072, 128], P('grp'), may hold values from -6 to 6
- codebook: bfloat16 [256, 128], replicated, may hold values from -4 to 4
- slot_codes: int32 [512, 4096], P('wide', 'grp'), may hold values from 0 to 255
- slot_centroid: int32 [512, 128], P('wide', 'grp'), may hold values from 0 to 131071, as said below
- lengths: int32 [512], P('wide'), may hold values from 1 to 128, 40960 in all
- candidates: int32 [256, 256], P(('grp', 'wide')), may hold values from 0 to 511, all different within a row
Outputs:
- scores: float32 [256, 256], P(('grp', 'wide'))
The draws below stay inside these ranges and needn't reach their ends.
Inputs may be any that keep to these rules, and one draw needn't show every extreme that they name: `slot_centroid`: the centroid of slot j of any passage lies in [(j // 32) * 32768, (j // 32 + 1) * 32768). `candidates`: each row names 256 different passages.
All inputs are finite; a program needn't handle non-finite values. No bound on the sum of `lengths` on one device may be relied on, other than what follows from the above.
Results may differ from the reference program's by a relative error of at most 0.00034.
Values may be sent and summed in bfloat16 or wider, within the bound.
No kernel may reach another device: no remote copies, remote signals or barrier semaphores. Data moves between devices by JAX's collectives and lax.ppermute only.
A program may use at most 64 MiB of HBM per device.

```python
import math
import jax
import jax.numpy as jnp
import numpy as np
from jax import lax

DIM = 128
QLEN = 32
L = 128
CODES = 256
NCENT = 131072
P_DEV = 4
NSUB = 32
NC_DEV = 32768
LQ = 32
Q = 256
P_SIZE = 512
CAND = 256


def draw_slot_centroid(key, part):
    key = jax.random.fold_in(key, 7)
    local_ids = jax.random.randint(key, (P_SIZE, L), 0, NC_DEV, dtype=jnp.int32)
    offsets = jnp.arange(L, dtype=jnp.int32) // LQ * NC_DEV
    return local_ids + offsets[None, :]


def with_ends(array, stream_key, smallest, top_value):
    longest = array.shape.index(max(array.shape))
    spots = []
    for shift in (0, 1):
        where = [jax.random.randint(jax.random.fold_in(stream_key, axis), (), 0, length) for axis, length in enumerate(array.shape)]
        where[longest] = (where[longest] + shift) % array.shape[longest]
        spots.append(tuple(where))
    return array.at[spots[0]].set(smallest).at[spots[1]].set(top_value)


def block_levels(stream_key, extent, cuts, least, top_value):
    factor_of = 1.0
    for dim, blocks in cuts:
        steps = jax.random.uniform(jax.random.fold_in(jax.random.fold_in(stream_key, 6), dim), (blocks,), jnp.float32, least / len(cuts), top_value / len(cuts))
        factor_of = factor_of * jnp.repeat(jnp.exp(steps), extent[dim] // blocks).reshape((-1,) + (1,) * (len(extent) - 1 - dim))
    return factor_of


def picks_of(own_key, rows, amount, top, lift):
    sequence = jax.random.permutation(jax.random.fold_in(own_key, 1), amount)
    favour = sequence
    for power in range(3):
        favour = favour * favour // amount
    favour = favour * lift // amount
    tickets = jax.random.randint(jax.random.fold_in(own_key, 2), (rows, amount), 0, 4096) + favour
    holders = jax.random.permutation(jax.random.fold_in(own_key, 3), rows)[jnp.arange(amount) % rows]
    tickets = jnp.where(jnp.arange(rows)[:, None] == holders[None, :], 1 << 14, tickets)
    merit = tickets * amount + jnp.arange(amount)
    return lax.top_k(merit.astype(jnp.int32), top)[1].astype(jnp.int32)


def profile(count, total, limit, skew):
    loads = [(1 << 20) // math.isqrt(standing ** skew) + 1 for standing in range(2, count + 1)]
    spare, counts = total - limit - (count - 1), [1] * (count - 1)
    while spare > 0:
        free = [i for i in range(count - 1) if counts[i] < limit]
        mass, left = sum([loads[i] for i in free]), spare
        for i in free:
            extra = min(limit - counts[i], max(1, left * loads[i] // mass), spare)
            counts[i] = counts[i] + extra
            spare = spare - extra
    return np.array([limit] + counts)


def uneven(rng, amount, total, bound, skew):
    if amount == 2:
        one = jax.random.randint(rng, (), max(1, total - bound), min(bound, total - 1) + 1)
        return jnp.stack([one, total - one])
    sizes = jnp.asarray(profile(amount, total, bound, skew), jnp.int32)
    couples = (amount - 1) // 2
    donor, receiver = sizes[1:1 + 2 * couples:2], sizes[2:2 + 2 * couples:2]
    margin = jnp.minimum(donor - 1, bound - receiver)
    moved = jax.random.randint(jax.random.fold_in(rng, 1), (couples,), 0, 1 << 20) % (margin + 1)
    sizes = sizes.at[1:1 + 2 * couples:2].set(donor - moved).at[2:2 + 2 * couples:2].set(receiver + moved)
    return sizes[jax.random.permutation(jax.random.fold_in(rng, 2), amount)]


def noise(stream_key, dims, deviation, limit, split=(), kind=jnp.bfloat16):
    factor_of = block_levels(stream_key, dims, split, -0.22, 0.18) if split else 1.0
    values = jax.random.normal(stream_key, dims, jnp.float32) * deviation * factor_of
    return jnp.minimum(jnp.maximum(values, -limit), limit).astype(kind)


def setup_inputs(seed: int = 0) -> dict:
    arg_keys = jax.random.split(jax.random.key(seed), 8)
    queries = noise(arg_keys[0], (Q, QLEN, DIM), 1.0, 6.0, ((0, 128),))
    centroids = noise(arg_keys[1], (NCENT, DIM), 1.0, 6.0, ((0, 4),))
    codebook = noise(arg_keys[2], (CODES, DIM), 0.6, 4.0)
    slot_codes = with_ends(jax.random.randint(arg_keys[3], (P_SIZE, L * NSUB), 0, CODES), jax.random.fold_in(arg_keys[3], 1), 0, CODES - 1).astype(jnp.int32)
    slot_centroid = draw_slot_centroid(jax.random.fold_in(arg_keys[7], 71), 0)
    lengths = uneven(arg_keys[5], P_SIZE, P_SIZE * L * 5 // 8, L, 2).astype(jnp.int32)
    candidates = picks_of(arg_keys[6], Q, P_SIZE, CAND, 8192)
    return {"queries": queries, "centroids": centroids, "codebook": codebook, "slot_codes": slot_codes, "slot_centroid": slot_centroid, "lengths": lengths, "candidates": candidates}


def unit_rows(values):
    wide32 = values.astype(jnp.float32)
    scale = lax.rsqrt(lax.optimization_barrier(jnp.sum(wide32 * wide32, axis=-1, keepdims=True)) + 1e-06)
    return (wide32 * scale).astype(jnp.bfloat16)

def reference(queries, centroids, codebook, slot_codes, slot_centroid, lengths, candidates):
    query_vecs = unit_rows(queries).astype(jnp.float32).reshape(Q * QLEN, DIM)
    code_table = codebook.astype(jnp.float32)
    columns = jnp.arange(DIM, dtype=jnp.int32)[None, :]

    def score_block(block_index):
        first = (block_index * P_DEV).astype(jnp.int32)
        block_codes = lax.dynamic_slice_in_dim(slot_codes, first, P_DEV, 0).reshape(P_DEV * L, NSUB)
        block_cent = lax.dynamic_slice_in_dim(slot_centroid, first, P_DEV, 0).reshape(P_DEV * L)
        block_len = lax.dynamic_slice_in_dim(lengths, first, P_DEV, 0)
        code_index = jnp.repeat(block_codes, 4, axis=1)
        residual = code_table[code_index, columns]
        raw = centroids[block_cent].astype(jnp.float32) + residual
        passage_vecs = unit_rows(raw).astype(jnp.float32)
        similar = jnp.dot(query_vecs, passage_vecs.T, precision=lax.Precision.HIGHEST)
        similar = similar.reshape(Q * QLEN, P_DEV, L)
        live_mask = jnp.arange(L, dtype=jnp.int32)[None, :] < block_len[:, None]
        best = lax.optimization_barrier(jnp.max(jnp.where(live_mask[None], similar, -1e+30), axis=2))
        return lax.optimization_barrier(jnp.sum(best.reshape(Q, QLEN, P_DEV), axis=1))
    blocks = lax.map(score_block, jnp.arange(P_SIZE // P_DEV, dtype=jnp.int32))
    table = jnp.transpose(blocks, (1, 0, 2)).reshape(Q, P_SIZE)
    return jnp.take_along_axis(table, candidates, axis=1)
```

```python
import functools

import jax
import jax.numpy as jnp
from jax import lax
from jax.experimental import pallas as pl
from jax.experimental.pallas import tpu as pltpu
from jax.sharding import PartitionSpec as P

SLAB = 16
LANES = 128
NT = (((1,), (1,)), ((), ()))


def unit(values):
    scale = lax.rsqrt(jnp.sum(values * values, axis=-1, keepdims=True) + 1e-06)
    return (values * scale).astype(jnp.bfloat16)


def decode_kernel(ids_smem, ids_ref, codes_ref, codebook_ref, centroids_ref, out_ref, slabs, sem):
    passages, slots = ids_ref.shape
    rows = passages * slots
    per_tile = 4
    tiles = slots // per_tile
    count = centroids_ref.shape[0]

    def start_passage(p, carry):
        for j in range(slots):
            row = (j % per_tile) * tiles * passages + (j // per_tile) * passages + p
            local = ids_smem[p, j] & (count - 1)
            base = pl.multiple_of(local & ~(SLAB - 1), SLAB)
            pltpu.make_async_copy(
                centroids_ref.at[pl.ds(base, SLAB), :], slabs.at[pl.ds(row * SLAB, SLAB), :], sem
            ).start()
        return carry

    lax.fori_loop(0, passages, start_passage, 0)

    table = codebook_ref[...].astype(jnp.float32)
    low, high = table[:LANES].T, table[LANES:].T
    codes = codes_ref[...].astype(jnp.float32).astype(jnp.bfloat16)
    stacked = jnp.concatenate(
        [codes[:, c * LANES : (c + 1) * LANES] for c in range(tiles)], axis=0
    )
    feature = lax.broadcasted_iota(jnp.int32, (LANES, LANES), 0)
    lane = lax.broadcasted_iota(jnp.int32, (LANES, LANES), 1)
    residuals = []
    for jj in range(per_tile):
        spread = (lane == jj * 32 + feature // 4).astype(jnp.float32).astype(jnp.bfloat16)
        index = lax.dot_general(spread, stacked, NT, preferred_element_type=jnp.float32)
        index = index.astype(jnp.int32)
        within = index & (LANES - 1)
        parts = []
        for s in range(0, LANES, 8):
            w = within[s : s + 8]
            first = jnp.take_along_axis(low[s : s + 8], w, axis=1)
            second = jnp.take_along_axis(high[s : s + 8], w, axis=1)
            parts.append(jnp.where(index[s : s + 8] < LANES, first, second))
        residuals.append(jnp.concatenate(parts, axis=0).T)

    pltpu.make_async_copy(centroids_ref.at[pl.ds(0, rows * SLAB), :], slabs, sem).wait()

    span = passages * SLAB
    column = lax.broadcasted_iota(jnp.int32, (passages, span), 1)
    first_row = lax.broadcasted_iota(jnp.int32, (passages, span), 0) * SLAB
    ids = ids_ref[...] & (SLAB - 1)
    for jj in range(per_tile):
        for c in range(tiles):
            j = c * per_tile + jj
            block = jj * tiles + c
            pick = (column == first_row + ids[:, j : j + 1]).astype(jnp.float32).astype(jnp.bfloat16)
            centre = jnp.dot(
                pick, slabs[block * span : (block + 1) * span, :], preferred_element_type=jnp.float32
            )
            raw = centre + residuals[jj][c * passages : (c + 1) * passages]
            out_ref[block * passages : (block + 1) * passages, :] = unit(raw)


def decode(slot_centroid, slot_codes, codebook, centroids):
    passages, slots = slot_centroid.shape
    rows, feature = passages * slots, codebook.shape[1]
    vmem = pl.BlockSpec(memory_space=pltpu.VMEM)
    return pl.pallas_call(
        decode_kernel,
        out_shape=jax.ShapeDtypeStruct((rows, feature), jnp.bfloat16),
        in_specs=[
            pl.BlockSpec(memory_space=pltpu.SMEM),
            vmem,
            vmem,
            vmem,
            pl.BlockSpec(memory_space=pl.ANY),
        ],
        out_specs=vmem,
        scratch_shapes=[
            pltpu.VMEM((rows * SLAB, feature), jnp.bfloat16),
            pltpu.SemaphoreType.DMA,
        ],
        compiler_params=pltpu.CompilerParams(vmem_limit_bytes=16 << 20),
        cost_estimate=pl.CostEstimate(
            flops=2 * rows * 256 * feature, bytes_accessed=rows * SLAB * 256, transcendentals=rows
        ),
        name="decode",
    )(slot_centroid, slot_centroid, slot_codes, codebook, centroids)


def score_kernel(per_tile, lengths_ref, queries_ref, vecs_ref, out_ref, unit_queries, live):
    blocks, rows, feature = vecs_ref.shape
    passages = lengths_ref.shape[0]
    slots = rows // passages
    tiles = slots // per_tile
    tokens = queries_ref.shape[0]
    owners = out_ref.shape[0]
    query_len = 32
    own = tokens // query_len // owners

    unit_queries[...] = unit(queries_ref[...].astype(jnp.float32))
    lengths = lengths_ref[...]
    first = vecs_ref[0, 0:passages, :]
    for b in range(blocks):
        for m in range(slots):
            j = b * slots + (m % tiles) * per_tile + m // tiles
            rows_here = vecs_ref[b, m * passages : (m + 1) * passages, :]
            if j:
                rows_here = jnp.where(lengths > j, rows_here, first)
            at = b * rows + m * passages
            live[at : at + passages, :] = rows_here

    chunk, span = 256, 256
    total = blocks * rows
    here = chunk // query_len
    segment = (
        lax.broadcasted_iota(jnp.int32, (here, chunk), 1) // query_len
        == lax.broadcasted_iota(jnp.int32, (here, chunk), 0)
    ).astype(jnp.float32)
    for k in range(tokens // chunk):
        wanted = unit_queries[k * chunk : (k + 1) * chunk, :]
        best = None
        for s in range(0, total, span):
            similar = lax.dot_general(
                live[s : s + span, :], wanted, NT, preferred_element_type=jnp.float32
            )
            top = jnp.max(similar.reshape(span // passages, passages, chunk), axis=0)
            best = top if best is None else jnp.maximum(best, top)
        scored = lax.dot_general(
            segment, best, NT, preferred_element_type=jnp.float32, precision=lax.Precision.HIGHEST
        )
        for i in range(here // own):
            out_ref[k * (here // own) + i, 0:own, 0:passages] = scored[i * own : (i + 1) * own]


def score(lengths, queries, vecs, owners, per_tile):
    blocks, rows, feature = vecs.shape
    tokens = queries.shape[0]
    vmem = pl.BlockSpec(memory_space=pltpu.VMEM)
    return pl.pallas_call(
        functools.partial(score_kernel, per_tile),
        out_shape=jax.ShapeDtypeStruct((owners, 8, LANES), jnp.float32),
        in_specs=[vmem, vmem, vmem],
        out_specs=vmem,
        scratch_shapes=[
            pltpu.VMEM((tokens, feature), jnp.bfloat16),
            pltpu.VMEM((blocks * rows, feature), jnp.bfloat16),
        ],
        compiler_params=pltpu.CompilerParams(vmem_limit_bytes=32 << 20),
        cost_estimate=pl.CostEstimate(
            flops=2 * tokens * blocks * rows * feature,
            bytes_accessed=(tokens + blocks * rows) * feature * 2,
            transcendentals=tokens,
        ),
        name="score",
    )(lengths, queries, vecs)


def pick_kernel(passages, owned_ref, candidates_ref, out_ref):
    owners = owned_ref.shape[0]
    count, wanted = candidates_ref.shape
    rows = lax.broadcasted_iota(jnp.int32, (owners, LANES), 0)
    for q in range(count):
        held = owned_ref[:, q, :]
        for c in range(0, wanted, LANES):
            ids = candidates_ref[q : q + 1, c : c + LANES]
            lane = jnp.broadcast_to(ids % passages, (owners, LANES))
            part = jnp.broadcast_to(ids // passages, (owners, LANES))
            found = jnp.take_along_axis(held, lane, axis=1)
            out_ref[q : q + 1, c : c + LANES] = jnp.sum(
                jnp.where(rows == part, found, 0.0), axis=0, keepdims=True
            )


def pick(owned, candidates, passages):
    vmem = pl.BlockSpec(memory_space=pltpu.VMEM)
    return pl.pallas_call(
        functools.partial(pick_kernel, passages),
        out_shape=jax.ShapeDtypeStruct(candidates.shape, jnp.float32),
        in_specs=[vmem, vmem],
        out_specs=vmem,
        name="pick",
    )(owned, candidates)


def shards(queries, centroids, codebook, slot_codes, slot_centroid, lengths, candidates):
    own, query_len, feature = queries.shape
    owners = lax.axis_size("wide")
    passages = lengths.shape[0]
    sent = jnp.broadcast_to(queries.reshape(1, own * query_len, feature), (owners, own * query_len, feature))
    gathered = lax.all_to_all(sent, "wide", split_axis=0, concat_axis=0, tiled=True)
    vecs = decode(slot_centroid, slot_codes, codebook, centroids)
    whole = lax.all_gather(vecs, "grp")
    table = score(
        lengths.reshape(passages, 1), gathered.reshape(owners * own * query_len, feature), whole, owners, 4
    )
    owned = lax.all_to_all(table, "wide", split_axis=0, concat_axis=0, tiled=True)
    return pick(owned, candidates, passages)


def solution(mesh):
    placed = (
        P(("grp", "wide"), None, None),
        P("grp", None),
        P(),
        P("wide", "grp"),
        P("wide", "grp"),
        P("wide"),
        P(("grp", "wide"), None),
    )
    return jax.shard_map(
        shards, mesh=mesh, in_specs=placed, out_specs=P(("grp", "wide"), None), check_vma=False
    )
```

```python
import functools

import jax
import jax.numpy as jnp
from jax import lax
from jax.experimental import pallas as pl
from jax.experimental.pallas import tpu as pltpu
from jax.sharding import PartitionSpec as P

SLAB = 16
LANES = 128
PER_TILE = 4
PIECES = 4
LOWEST = -1e30
NT = (((1,), (1,)), ((), ()))
VMEM = pl.BlockSpec(memory_space=pltpu.VMEM)
ANY = pl.BlockSpec(memory_space=pl.ANY)


def unit(values):
    scale = lax.rsqrt(jnp.sum(values * values, axis=-1, keepdims=True) + 1e-06)
    return (values * scale).astype(jnp.bfloat16)


def spread_kernel(queries_ref, out_ref):
    held = queries_ref[...]
    for i in range(out_ref.shape[0]):
        out_ref[i] = held


def spread(queries, owners):
    return pl.pallas_call(
        spread_kernel,
        out_shape=jax.ShapeDtypeStruct((owners, *queries.shape), queries.dtype),
        in_specs=[VMEM],
        out_specs=VMEM,
        compiler_params=params(4),
        cost_estimate=pl.CostEstimate(flops=20000000000, bytes_accessed=1000000, transcendentals=0),
        name="spread",
    )(queries)


def residual_rows(codes, codebook, store):
    tiles = codes.shape[1] // LANES
    table = codebook.astype(jnp.float32)
    low, high = table[:LANES].T, table[LANES:].T
    codes = codes.astype(jnp.float32).astype(jnp.bfloat16)
    stacked = jnp.concatenate(
        [codes[:, c * LANES : (c + 1) * LANES] for c in range(tiles)], axis=0
    )
    feature = lax.broadcasted_iota(jnp.int32, (LANES, LANES), 0)
    lane = lax.broadcasted_iota(jnp.int32, (LANES, LANES), 1)
    for jj in range(PER_TILE):
        pattern = (lane == jj * 32 + feature // 4).astype(jnp.float32).astype(jnp.bfloat16)
        index = lax.dot_general(pattern, stacked, NT, preferred_element_type=jnp.float32)
        index = index.astype(jnp.int32)
        within = index & (LANES - 1)
        parts = []
        for s in range(0, LANES, 8):
            w = within[s : s + 8]
            first = jnp.take_along_axis(low[s : s + 8], w, axis=1)
            second = jnp.take_along_axis(high[s : s + 8], w, axis=1)
            parts.append(jnp.where(index[s : s + 8] < LANES, first, second))
        store(jj, jnp.concatenate(parts, axis=0).T)


def decode_kernel(
    ids_hbm, lengths_hbm, codes_hbm, book_hbm, cent_hbm, out_ref, live_ref,
    ids, lengths, codes, book, table, residual, sems,
):
    passages, slots = ids.shape
    tiles = slots // PER_TILE
    count = table.shape[0]
    copies = [
        pltpu.make_async_copy(source, target, sems.at[i])
        for i, (source, target) in enumerate(
            [(codes_hbm, codes), (book_hbm, book), (ids_hbm, ids), (lengths_hbm, lengths)]
        )
    ]
    piece = count // PIECES
    for i in range(PIECES):
        part = pl.ds(i * piece, piece)
        copies.append(pltpu.make_async_copy(cent_hbm.at[part, :], table.at[part, :], sems.at[4 + i]))
    for copy in copies:
        copy.start()
    for copy in copies[:4]:
        copy.wait()

    row = lax.broadcasted_iota(jnp.int32, (passages, LANES), 0)
    live = jnp.zeros((passages, LANES), jnp.int32)
    for p in range(passages):
        live = jnp.where(row == p, lengths[p], live)
    live_ref[...] = live

    def store(jj, rows):
        residual[jj * LANES : (jj + 1) * LANES, :] = rows

    residual_rows(codes[...], book[...], store)
    for copy in copies[4:]:
        copy.wait()

    sublane = lax.broadcasted_iota(jnp.int32, (8, LANES), 0)

    def gather(m, carry):
        j = (m % tiles) * PER_TILE + m // tiles
        halves = []
        for h in range(0, passages, 8):
            held = jnp.zeros((8, LANES), jnp.float32)
            for q in range(8):
                local = ids[h + q, j] & (count - 1)
                base = pl.multiple_of(local & ~(SLAB - 1), SLAB)
                slab = table[pl.ds(base, SLAB), :].astype(jnp.float32)
                within = local & (SLAB - 1)
                half = jnp.where(within >= 8, slab[8:], slab[:8])
                held = jnp.where(sublane == q, pltpu.roll(half, (q - within) & 7, 0), held)
            halves.append(held)
        at = pl.multiple_of(m * passages, passages)
        raw = jnp.concatenate(halves, axis=0) + residual[pl.ds(at, passages), :]
        out_ref[pl.ds(at, passages), :] = unit(raw)
        return carry

    lax.fori_loop(0, slots, gather, 0, unroll=8)


def decode(slot_centroid, lengths, slot_codes, codebook, centroids):
    passages, slots = slot_centroid.shape
    rows, feature = passages * slots, codebook.shape[1]
    return pl.pallas_call(
        decode_kernel,
        out_shape=(
            jax.ShapeDtypeStruct((rows, feature), jnp.bfloat16),
            jax.ShapeDtypeStruct((passages, LANES), jnp.int32),
        ),
        in_specs=[ANY] * 5,
        out_specs=(VMEM, VMEM),
        scratch_shapes=[
            pltpu.SMEM(slot_centroid.shape, jnp.int32),
            pltpu.SMEM(lengths.shape, jnp.int32),
            pltpu.VMEM(slot_codes.shape, jnp.int32),
            pltpu.VMEM(codebook.shape, jnp.bfloat16),
            pltpu.VMEM(centroids.shape, jnp.bfloat16),
            pltpu.VMEM((rows, feature), jnp.float32),
            pltpu.SemaphoreType.DMA((4 + PIECES,)),
        ],
        compiler_params=pltpu.CompilerParams(vmem_limit_bytes=57 << 20),
        cost_estimate=pl.CostEstimate(
            flops=2 * rows * 256 * feature, bytes_accessed=centroids.size * 2, transcendentals=rows
        ),
        name="decode",
    )(slot_centroid, lengths, slot_codes, codebook, centroids)


def maxima(live, tokens, blocks, scratch, store):
    passages = live.shape[0]
    rows = scratch.shape[0] // len(blocks)
    slots = rows // passages
    tiles = slots // PER_TILE
    for b, (begin, vecs) in enumerate(blocks):
        first = vecs[0:passages, :]
        for m in range(slots):
            j = (m % tiles) * PER_TILE + m // tiles
            held = vecs[m * passages : (m + 1) * passages, :]
            if j:
                held = jnp.where(live > begin + j, held, first)
            at = b * rows + m * passages
            scratch[at : at + passages, :] = held

    chunk, span = 1024, 128
    for k in range(0, tokens.shape[0], chunk):
        wanted = tokens[k : k + chunk, :]
        best = None
        for b, (begin, _) in enumerate(blocks):
            top = None
            for s in range(b * rows, (b + 1) * rows, span):
                similar = lax.dot_general(
                    scratch[s : s + span, :], wanted, NT, preferred_element_type=jnp.float32
                )
                here = jnp.max(similar.reshape(span // passages, passages, chunk), axis=0)
                top = here if top is None else jnp.maximum(top, here)
            top = jnp.where(live[:, :1] > begin, top, LOWEST)
            best = top if best is None else jnp.maximum(best, top)
        store(k, best)


def score_kernel(live, queries, vecs, out_ref, scratch, whole, tokens):
    passages, count = live.shape[0], queries.shape[0]
    owners = out_ref.shape[0]
    own = 2
    query_len = count // owners // own
    slots = vecs.shape[1] // passages
    tokens[...] = unit(queries[...].astype(jnp.float32))

    def store(k, best):
        high = best.astype(jnp.bfloat16)
        rest = best - high.astype(jnp.float32)
        mid = rest.astype(jnp.bfloat16)
        low = (rest - mid.astype(jnp.float32)).astype(jnp.bfloat16)
        for i, part in enumerate((high, mid, low)):
            whole[i * passages : (i + 1) * passages, k : k + best.shape[1]] = part

    maxima(live[...], tokens, [(b * slots, vecs.at[b]) for b in range(4)], scratch, store)
    token = lax.broadcasted_iota(jnp.int32, (owners, count), 1) // query_len
    owner = lax.broadcasted_iota(jnp.int32, (owners, count), 0)
    for q in range(own):
        members = (token == owner * own + q).astype(jnp.float32).astype(jnp.bfloat16)
        sums = lax.dot_general(members, whole[...], NT, preferred_element_type=jnp.float32)
        total = sums[:, 2 * passages : 3 * passages] + sums[:, passages : 2 * passages]
        out_ref[:, q * passages : (q + 1) * passages] = total + sums[:, :passages]


def params(mebibytes):
    return pltpu.CompilerParams(vmem_limit_bytes=mebibytes << 20)


def cost(tokens, rows, feature):
    return pl.CostEstimate(
        flops=2 * tokens * rows * feature,
        bytes_accessed=(tokens + rows) * feature * 2,
        transcendentals=tokens,
    )


def shards(queries, centroids, codebook, slot_codes, slot_centroid, lengths, candidates):
    own, query_len, feature = queries.shape
    owners = lax.axis_size("wide")
    passages = lengths.shape[0]
    tokens = owners * own * query_len
    rows = slot_centroid.size
    sent = spread(queries.reshape(own * query_len, feature), owners)
    gathered = lax.all_to_all(sent, "wide", split_axis=0, concat_axis=0, tiled=True)
    gathered = gathered.reshape(tokens, feature)
    vecs, live = decode(slot_centroid, lengths, slot_codes, codebook, centroids)

    whole = lax.all_gather(vecs, "grp")
    table = pl.pallas_call(
        score_kernel,
        out_shape=jax.ShapeDtypeStruct((owners, LANES), jnp.float32),
        in_specs=[VMEM] * 3,
        out_specs=VMEM,
        scratch_shapes=[
            pltpu.VMEM((4 * rows, feature), jnp.bfloat16),
            pltpu.VMEM((3 * passages, tokens), jnp.bfloat16),
            pltpu.VMEM((tokens, feature), jnp.bfloat16),
        ],
        compiler_params=params(24),
        cost_estimate=cost(tokens, 4 * rows, feature),
        name="score",
    )(live, gathered, whole)
    owned = lax.all_to_all(table, "wide", split_axis=0, concat_axis=0, tiled=True)
    return pick(owned, candidates, passages)


def pick_kernel(passages, owned_ref, candidates_ref, out_ref):
    owners = owned_ref.shape[0]
    count, wanted = candidates_ref.shape
    rows = lax.broadcasted_iota(jnp.int32, (owners, LANES), 0)
    held = owned_ref[...]
    for q in range(count):
        for c in range(0, wanted, LANES):
            ids = candidates_ref[q : q + 1, c : c + LANES]
            lane = jnp.broadcast_to(q * passages + ids % passages, (owners, LANES))
            part = jnp.broadcast_to(ids // passages, (owners, LANES))
            found = jnp.take_along_axis(held, lane, axis=1)
            out_ref[q : q + 1, c : c + LANES] = jnp.sum(
                jnp.where(rows == part, found, 0.0), axis=0, keepdims=True
            )


def pick(owned, candidates, passages):
    return pl.pallas_call(
        functools.partial(pick_kernel, passages),
        out_shape=jax.ShapeDtypeStruct(candidates.shape, jnp.float32),
        in_specs=[VMEM, VMEM],
        out_specs=VMEM,
        compiler_params=params(2),
        cost_estimate=pl.CostEstimate(
            flops=candidates.size * owned.shape[0] * 2, bytes_accessed=owned.size * 4, transcendentals=0
        ),
        name="pick",
    )(owned, candidates)


def solution(mesh):
    placed = (
        P(("grp", "wide"), None, None),
        P("grp", None),
        P(),
        P("wide", "grp"),
        P("wide", "grp"),
        P("wide"),
        P(("grp", "wide"), None),
    )
    return jax.shard_map(
        shards, mesh=mesh, in_specs=placed, out_specs=P(("grp", "wide"), None), check_vma=False
    )
```

```python
import functools

import jax
import jax.numpy as jnp
from jax import lax
from jax.experimental import pallas as pl
from jax.experimental.pallas import tpu as pltpu
from jax.sharding import PartitionSpec as P

SLAB = 16
LANES = 128
PER_TILE = 4
PIECES = 4
LOWEST = -1e30
PAIR = 4
NT = (((1,), (1,)), ((), ()))
VMEM = pl.BlockSpec(memory_space=pltpu.VMEM)
ANY = pl.BlockSpec(memory_space=pl.ANY)


def unit(values):
    scale = lax.rsqrt(jnp.sum(values * values, axis=-1, keepdims=True) + 1e-06)
    return (values * scale).astype(jnp.bfloat16)


def unit_kernel(queries, out):
    out[...] = unit(queries[...].astype(jnp.float32))


def unit_queries(queries):
    return pl.pallas_call(
        unit_kernel,
        out_shape=jax.ShapeDtypeStruct(queries.shape, jnp.bfloat16),
        in_specs=[VMEM],
        out_specs=VMEM,
        compiler_params=params(2),
        cost_estimate=pl.CostEstimate(flops=20000000000, bytes_accessed=queries.size * 2, transcendentals=0),
        name="unit_queries",
    )(queries)


def spread_kernel(queries_ref, partner_ref, after_ref, out_ref):
    rows = queries_ref.shape[0]
    low = (lax.axis_index("wide") & PAIR) == 0
    own, partner = queries_ref[...], partner_ref[...]
    first, second = jnp.where(low, own, partner), jnp.where(low, partner, own)
    for i in range(out_ref.shape[0]):
        out_ref[i, 0:rows, :] = first
        out_ref[i, rows : 2 * rows, :] = second


def spread(queries, partner, after, count):
    rows, feature = queries.shape
    return pl.pallas_call(
        spread_kernel,
        out_shape=jax.ShapeDtypeStruct((count, 2 * rows, feature), queries.dtype),
        in_specs=[VMEM, VMEM, ANY],
        out_specs=VMEM,
        compiler_params=params(4),
        cost_estimate=pl.CostEstimate(flops=0, bytes_accessed=count * rows * feature * 4, transcendentals=0),
        name="spread",
    )(queries, partner, after)


def residual_rows(codes, codebook, store):
    tiles = codes.shape[1] // LANES
    table = codebook.astype(jnp.float32)
    low, high = table[:LANES].T, table[LANES:].T
    codes = codes.astype(jnp.float32).astype(jnp.bfloat16)
    stacked = jnp.concatenate(
        [codes[:, c * LANES : (c + 1) * LANES] for c in range(tiles)], axis=0
    )
    feature = lax.broadcasted_iota(jnp.int32, (LANES, LANES), 0)
    lane = lax.broadcasted_iota(jnp.int32, (LANES, LANES), 1)
    for jj in range(PER_TILE):
        pattern = (lane == jj * 32 + feature // 4).astype(jnp.float32).astype(jnp.bfloat16)
        index = lax.dot_general(pattern, stacked, NT, preferred_element_type=jnp.float32)
        index = index.astype(jnp.int32)
        within = index & (LANES - 1)
        parts = []
        for s in range(0, LANES, 8):
            w = within[s : s + 8]
            first = jnp.take_along_axis(low[s : s + 8], w, axis=1)
            second = jnp.take_along_axis(high[s : s + 8], w, axis=1)
            parts.append(jnp.where(index[s : s + 8] < LANES, first, second))
        store(jj, jnp.concatenate(parts, axis=0).T)


def residual_kernel(codes, book, out):
    def store(jj, rows):
        out[jj * LANES : (jj + 1) * LANES, :] = rows

    residual_rows(codes[...], book[...], store)


def gather_kernel(ids, lengths, residual, table, out_ref, live_ref):
    passages, slots = ids.shape
    tiles = slots // PER_TILE
    count = table.shape[0]
    row = lax.broadcasted_iota(jnp.int32, (passages, LANES), 0)
    live = jnp.zeros((passages, LANES), jnp.int32)
    for p in range(passages):
        live = jnp.where(row == p, lengths[p], live)
    live_ref[...] = live
    sublane = lax.broadcasted_iota(jnp.int32, (8, LANES), 0)

    def gather(m, carry):
        j = (m % tiles) * PER_TILE + m // tiles
        halves = []
        for h in range(0, passages, 8):
            held = jnp.zeros((8, LANES), jnp.float32)
            for q in range(8):
                local = ids[h + q, j] & (count - 1)
                base = pl.multiple_of(local & ~(SLAB - 1), SLAB)
                slab = table[pl.ds(base, SLAB), :].astype(jnp.float32)
                within = local & (SLAB - 1)
                half = jnp.where(within >= 8, slab[8:], slab[:8])
                held = jnp.where(sublane == q, pltpu.roll(half, (q - within) & 7, 0), held)
            halves.append(held)
        at = pl.multiple_of(m * passages, passages)
        raw = jnp.concatenate(halves, axis=0) + residual[pl.ds(at, passages), :]
        out_ref[pl.ds(at, passages), :] = unit(raw)
        return carry

    lax.fori_loop(0, slots, gather, 0, unroll=8)


def decode(slot_centroid, lengths, slot_codes, codebook, centroids):
    passages, slots = slot_centroid.shape
    rows, feature = passages * slots, codebook.shape[1]
    smem = pl.BlockSpec(memory_space=pltpu.SMEM)
    residual = pl.pallas_call(
        residual_kernel,
        out_shape=jax.ShapeDtypeStruct((rows, feature), jnp.float32),
        in_specs=[VMEM, VMEM],
        out_specs=VMEM,
        compiler_params=params(4),
        cost_estimate=pl.CostEstimate(flops=rows * 256 * feature, bytes_accessed=rows * 256, transcendentals=0),
        name="residual",
    )(slot_codes, codebook)
    return pl.pallas_call(
        gather_kernel,
        out_shape=(
            jax.ShapeDtypeStruct((rows, feature), jnp.bfloat16),
            jax.ShapeDtypeStruct((passages, LANES), jnp.int32),
        ),
        in_specs=[smem, smem, VMEM, VMEM],
        out_specs=(VMEM, VMEM),
        compiler_params=params(4 + centroids.size * 2 // (1 << 20)),
        cost_estimate=pl.CostEstimate(
            flops=rows * feature * 8, bytes_accessed=centroids.size * 2, transcendentals=rows
        ),
        name="gather",
    )(slot_centroid, lengths, residual, centroids)


def maxima(live, tokens, blocks, scratch, store):
    passages = live.shape[0]
    rows = scratch.shape[0] // len(blocks)
    slots = rows // passages
    tiles = slots // PER_TILE
    for b, (begin, vecs) in enumerate(blocks):
        first = vecs[0:passages, :]
        for m in range(slots):
            j = (m % tiles) * PER_TILE + m // tiles
            held = vecs[m * passages : (m + 1) * passages, :]
            if j:
                held = jnp.where(live > begin + j, held, first)
            at = b * rows + m * passages
            scratch[at : at + passages, :] = held

    chunk, span = 1024, 128
    for k in range(0, tokens.shape[0], chunk):
        wanted = tokens[k : k + chunk, :]
        best = None
        for b, (begin, _) in enumerate(blocks):
            top = None
            for s in range(b * rows, (b + 1) * rows, span):
                similar = lax.dot_general(
                    scratch[s : s + span, :], wanted, NT, preferred_element_type=jnp.float32
                )
                here = jnp.max(similar.reshape(span // passages, passages, chunk), axis=0)
                top = here if top is None else jnp.maximum(top, here)
            top = jnp.where(live[:, :1] > begin, top, LOWEST)
            best = top if best is None else jnp.maximum(best, top)
        store(k, best)


def score_kernel(live, tokens, vecs, out_ref, scratch, whole):
    passages, count = live.shape[0], tokens.shape[0]
    owners = out_ref.shape[0]
    own = 2
    query_len = count // owners // own
    slots = vecs.shape[1] // passages

    def store(k, best):
        high = best.astype(jnp.bfloat16)
        rest = best - high.astype(jnp.float32)
        mid = rest.astype(jnp.bfloat16)
        low = (rest - mid.astype(jnp.float32)).astype(jnp.bfloat16)
        for i, part in enumerate((high, mid, low)):
            whole[i * passages : (i + 1) * passages, k : k + best.shape[1]] = part

    maxima(live[...], tokens, [(b * slots, vecs.at[b]) for b in range(4)], scratch, store)
    query = lax.broadcasted_iota(jnp.int32, (owners, count), 1) // query_len
    owner = lax.broadcasted_iota(jnp.int32, (owners, count), 0)
    pair = (owner // (2 * PAIR)) * PAIR + owner % PAIR
    place = pair * 2 + (owner // PAIR) % 2
    for q in range(own):
        members = (query == place * own + q).astype(jnp.float32).astype(jnp.bfloat16)
        sums = lax.dot_general(members, whole[...], NT, preferred_element_type=jnp.float32)
        total = sums[:, 2 * passages : 3 * passages] + sums[:, passages : 2 * passages]
        out_ref[:, q * passages : (q + 1) * passages] = total + sums[:, :passages]


def params(mebibytes):
    return pltpu.CompilerParams(vmem_limit_bytes=mebibytes << 20)


def cost(tokens, rows, feature):
    return pl.CostEstimate(
        flops=2 * tokens * rows * feature,
        bytes_accessed=(tokens + rows) * feature * 2,
        transcendentals=tokens,
    )


def shards(queries, centroids, codebook, slot_codes, slot_centroid, lengths, candidates):
    own, query_len, feature = queries.shape
    owners = lax.axis_size("wide")
    passages = lengths.shape[0]
    tokens = owners * own * query_len
    rows = slot_centroid.size
    plain = unit_queries(queries.reshape(own * query_len, feature))
    partner = lax.ppermute(plain, "wide", [(i, i ^ PAIR) for i in range(owners)])
    vecs, live = decode(slot_centroid, lengths, slot_codes, codebook, centroids)
    sent = spread(plain, partner, live, owners // 2)
    groups = [[i + z for i in range(owners) if not i & PAIR] for z in (0, PAIR)]
    gathered = lax.all_to_all(
        sent, "wide", split_axis=0, concat_axis=0, axis_index_groups=groups, tiled=True
    ).reshape(tokens, feature)

    whole = lax.all_gather(vecs, "grp")
    table = pl.pallas_call(
        score_kernel,
        out_shape=jax.ShapeDtypeStruct((owners, LANES), jnp.float32),
        in_specs=[VMEM] * 3,
        out_specs=VMEM,
        scratch_shapes=[
            pltpu.VMEM((4 * rows, feature), jnp.bfloat16),
            pltpu.VMEM((3 * passages, tokens), jnp.bfloat16),
        ],
        compiler_params=params(24),
        cost_estimate=cost(tokens, 4 * rows, feature),
        name="score",
    )(live, gathered, whole)
    owned = lax.all_to_all(table, "wide", split_axis=0, concat_axis=0, tiled=True)
    return pick(owned, candidates, passages)


def pick_kernel(passages, owned_ref, candidates_ref, out_ref):
    owners = owned_ref.shape[0]
    count, wanted = candidates_ref.shape
    rows = lax.broadcasted_iota(jnp.int32, (owners, LANES), 0)
    held = owned_ref[...]
    for q in range(count):
        for c in range(0, wanted, LANES):
            ids = candidates_ref[q : q + 1, c : c + LANES]
            lane = jnp.broadcast_to(q * passages + ids % passages, (owners, LANES))
            part = jnp.broadcast_to(ids // passages, (owners, LANES))
            found = jnp.take_along_axis(held, lane, axis=1)
            out_ref[q : q + 1, c : c + LANES] = jnp.sum(
                jnp.where(rows == part, found, 0.0), axis=0, keepdims=True
            )


def pick(owned, candidates, passages):
    return pl.pallas_call(
        functools.partial(pick_kernel, passages),
        out_shape=jax.ShapeDtypeStruct(candidates.shape, jnp.float32),
        in_specs=[VMEM, VMEM],
        out_specs=VMEM,
        compiler_params=params(2),
        cost_estimate=pl.CostEstimate(
            flops=candidates.size * owned.shape[0] * 2, bytes_accessed=owned.size * 4, transcendentals=0
        ),
        name="pick",
    )(owned, candidates)


def solution(mesh):
    placed = (
        P(("grp", "wide"), None, None),
        P("grp", None),
        P(),
        P("wide", "grp"),
        P("wide", "grp"),
        P("wide"),
        P(("grp", "wide"), None),
    )
    return jax.shard_map(
        shards, mesh=mesh, in_specs=placed, out_specs=P(("grp", "wide"), None), check_vma=False
    )
```

```python
import functools

import jax
import jax.numpy as jnp
from jax import lax
from jax.experimental import pallas as pl
from jax.experimental.pallas import tpu as pltpu
from jax.sharding import PartitionSpec as P

SLAB = 16
LANES = 128
PER_TILE = 4
PIECES = 4
LOWEST = -1e30
PAIR = 4
NT = (((1,), (1,)), ((), ()))
VMEM = pl.BlockSpec(memory_space=pltpu.VMEM)
ANY = pl.BlockSpec(memory_space=pl.ANY)


def unit(values):
    scale = lax.rsqrt(jnp.sum(values * values, axis=-1, keepdims=True) + 1e-06)
    return (values * scale).astype(jnp.bfloat16)


def members_kernel(query_len, out_ref):
    own, owners, count = out_ref.shape
    query = lax.broadcasted_iota(jnp.int32, (owners, count), 1) // query_len
    owner = lax.broadcasted_iota(jnp.int32, (owners, count), 0)
    pair = (owner // (2 * PAIR)) * PAIR + owner % PAIR
    place = pair * 2 + (owner // PAIR) % 2
    for q in range(own):
        out_ref[q] = (query == place * own + q).astype(jnp.float32).astype(jnp.bfloat16)


def members_of(own, owners, query_len):
    return pl.pallas_call(
        functools.partial(members_kernel, query_len),
        out_shape=jax.ShapeDtypeStruct((own, owners, owners * own * query_len), jnp.bfloat16),
        out_specs=VMEM,
        compiler_params=params(2),
        cost_estimate=pl.CostEstimate(flops=20000000000, bytes_accessed=1000, transcendentals=0),
        name="members",
    )()


def spread_kernel(queries_ref, partner_ref, out_ref):
    rows = queries_ref.shape[0]
    low = (lax.axis_index("wide") & PAIR) == 0
    own = unit(queries_ref[...].astype(jnp.float32))
    partner = unit(partner_ref[...].astype(jnp.float32))
    first, second = jnp.where(low, own, partner), jnp.where(low, partner, own)
    for i in range(out_ref.shape[0]):
        out_ref[i, 0:rows, :] = first
        out_ref[i, rows : 2 * rows, :] = second


def spread(queries, partner, count):
    rows, feature = queries.shape
    return pl.pallas_call(
        spread_kernel,
        out_shape=jax.ShapeDtypeStruct((count, 2 * rows, feature), queries.dtype),
        in_specs=[VMEM, VMEM],
        out_specs=VMEM,
        compiler_params=params(4),
        cost_estimate=pl.CostEstimate(flops=0, bytes_accessed=count * rows * feature * 4, transcendentals=0),
        name="spread",
    )(queries, partner)


def residual_rows(codes, codebook, store):
    tiles = codes.shape[1] // LANES
    table = codebook.astype(jnp.float32)
    low, high = table[:LANES].T, table[LANES:].T
    codes = codes.astype(jnp.float32).astype(jnp.bfloat16)
    stacked = jnp.concatenate(
        [codes[:, c * LANES : (c + 1) * LANES] for c in range(tiles)], axis=0
    )
    feature = lax.broadcasted_iota(jnp.int32, (LANES, LANES), 0)
    lane = lax.broadcasted_iota(jnp.int32, (LANES, LANES), 1)
    for jj in range(PER_TILE):
        pattern = (lane == jj * 32 + feature // 4).astype(jnp.float32).astype(jnp.bfloat16)
        index = lax.dot_general(pattern, stacked, NT, preferred_element_type=jnp.float32)
        index = index.astype(jnp.int32)
        within = index & (LANES - 1)
        parts = []
        for s in range(0, LANES, 8):
            w = within[s : s + 8]
            first = jnp.take_along_axis(low[s : s + 8], w, axis=1)
            second = jnp.take_along_axis(high[s : s + 8], w, axis=1)
            parts.append(jnp.where(index[s : s + 8] < LANES, first, second))
        store(jj, jnp.concatenate(parts, axis=0).T)


def residual_kernel(codes, book, lengths, out, live):
    def store(jj, rows):
        out[jj * LANES : (jj + 1) * LANES, :] = rows

    residual_rows(codes[...], book[...], store)
    count = live.shape[0]
    row = lax.broadcasted_iota(jnp.int32, (count, count), 0)
    lane = lax.broadcasted_iota(jnp.int32, (count, count), 1)
    held = jnp.where(row == lane, jnp.broadcast_to(lengths[...], (count, count)), 0)
    live[...] = jnp.broadcast_to(jnp.sum(held, axis=1, keepdims=True), live.shape)


def gather_kernel(ids, residual, table, out_ref):
    passages, slots = ids.shape
    tiles = slots // PER_TILE
    count = table.shape[0]
    sublane = lax.broadcasted_iota(jnp.int32, (8, LANES), 0)

    for m in range(slots):
        j = (m % tiles) * PER_TILE + m // tiles
        halves = []
        for h in range(0, passages, 8):
            held = jnp.zeros((8, LANES), jnp.float32)
            for q in range(8):
                local = ids[h + q, j] & (count - 1)
                base = pl.multiple_of(local & ~(SLAB - 1), SLAB)
                slab = table[pl.ds(base, SLAB), :].astype(jnp.float32)
                within = local & (SLAB - 1)
                half = jnp.where(within >= 8, slab[8:], slab[:8])
                held = jnp.where(sublane == q, pltpu.roll(half, (q - within) & 7, 0), held)
            halves.append(held)
        at = m * passages
        raw = jnp.concatenate(halves, axis=0) + residual[at : at + passages, :]
        out_ref[at : at + passages, :] = unit(raw)


def decode(slot_centroid, lengths, slot_codes, codebook, centroids, sent):
    passages, slots = slot_centroid.shape
    rows, feature = passages * slots, codebook.shape[1]
    smem = pl.BlockSpec(memory_space=pltpu.SMEM)
    residual, live = pl.pallas_call(
        residual_kernel,
        out_shape=(
            jax.ShapeDtypeStruct((rows, feature), jnp.float32),
            jax.ShapeDtypeStruct((passages, LANES), jnp.int32),
        ),
        in_specs=[VMEM] * 3,
        out_specs=(VMEM, VMEM),
        compiler_params=params(4),
        cost_estimate=pl.CostEstimate(flops=rows * 256 * feature, bytes_accessed=rows * 256, transcendentals=0),
        name="residual",
    )(slot_codes, codebook, lengths.reshape(1, passages))
    residual, sent = lax.optimization_barrier((residual, sent))
    vecs = pl.pallas_call(
        gather_kernel,
        out_shape=jax.ShapeDtypeStruct((rows, feature), jnp.bfloat16),
        in_specs=[smem, VMEM, VMEM],
        out_specs=VMEM,
        compiler_params=params(4 + centroids.size * 2 // (1 << 20)),
        cost_estimate=pl.CostEstimate(
            flops=rows * feature * 8, bytes_accessed=centroids.size * 2, transcendentals=rows
        ),
        name="gather",
    )(slot_centroid, residual, centroids)
    vecs, sent = lax.optimization_barrier((vecs, sent))
    return vecs, live, sent


def maxima(live, tokens, blocks, scratch, store):
    passages = live.shape[0]
    rows = scratch.shape[0] // len(blocks)
    slots = rows // passages
    tiles = slots // PER_TILE
    for b, (begin, vecs) in enumerate(blocks):
        first = vecs[0:passages, :]
        for m in range(slots):
            j = (m % tiles) * PER_TILE + m // tiles
            held = vecs[m * passages : (m + 1) * passages, :]
            if j:
                held = jnp.where(live > begin + j, held, first)
            at = b * rows + m * passages
            scratch[at : at + passages, :] = held

    chunk, span = 1024, 128
    for k in range(0, tokens.shape[0], chunk):
        wanted = tokens[k : k + chunk, :]
        best = None
        for b, (begin, _) in enumerate(blocks):
            top = None
            for s in range(b * rows, (b + 1) * rows, span):
                similar = lax.dot_general(
                    scratch[s : s + span, :], wanted, NT, preferred_element_type=jnp.float32
                )
                here = jnp.max(similar.reshape(span // passages, passages, chunk), axis=0)
                top = here if top is None else jnp.maximum(top, here)
            top = jnp.where(live[:, :1] > begin, top, LOWEST)
            best = top if best is None else jnp.maximum(best, top)
        store(k, best)


def begins(slots):
    own = lax.axis_index("grp")
    return [jnp.bitwise_xor(own, s) * slots for s in range(4)]


def near_kernel(live, tokens, own, other, best_out, scratch):
    begin = begins(own.shape[0] // live.shape[0])

    def store(k, best):
        best_out[:, k : k + best.shape[1]] = best

    maxima(live[...], tokens, [(begin[0], own), (begin[1], other)], scratch, store)


def far_kernel(live, tokens, vecs, before, best_out, scratch):
    begin = begins(vecs.shape[0] // live.shape[0])

    def store(k, best):
        best_out[:, k : k + best.shape[1]] = jnp.maximum(best, before[:, k : k + best.shape[1]])

    maxima(live[...], tokens, [(begin[2], vecs)], scratch, store)


def last_kernel(live, tokens, vecs, before, members, out_ref, scratch, whole):
    passages = live.shape[0]
    begin = begins(vecs.shape[0] // passages)

    def store(k, best):
        best = jnp.maximum(best, before[:, k : k + best.shape[1]])
        high = best.astype(jnp.bfloat16)
        rest = best - high.astype(jnp.float32)
        mid = rest.astype(jnp.bfloat16)
        low = (rest - mid.astype(jnp.float32)).astype(jnp.bfloat16)
        for i, part in enumerate((high, mid, low)):
            whole[i * passages : (i + 1) * passages, k : k + best.shape[1]] = part

    maxima(live[...], tokens, [(begin[3], vecs)], scratch, store)
    for q in range(members.shape[0]):
        sums = lax.dot_general(members[q], whole[...], NT, preferred_element_type=jnp.float32)
        total = sums[:, 2 * passages : 3 * passages] + sums[:, passages : 2 * passages]
        out_ref[:, q * passages : (q + 1) * passages] = total + sums[:, :passages]


def params(mebibytes):
    return pltpu.CompilerParams(vmem_limit_bytes=mebibytes << 20)


def cost(tokens, rows, feature):
    return pl.CostEstimate(
        flops=2 * tokens * rows * feature,
        bytes_accessed=(tokens + rows) * feature * 2,
        transcendentals=tokens,
    )


def shards(queries, centroids, codebook, slot_codes, slot_centroid, lengths, candidates):
    own, query_len, feature = queries.shape
    owners = lax.axis_size("wide")
    passages = lengths.shape[0]
    tokens = owners * own * query_len
    rows = slot_centroid.size
    plain = queries.reshape(own * query_len, feature)
    members = members_of(own, owners, query_len)
    members, slot_codes = lax.optimization_barrier((members, slot_codes))
    partner = lax.ppermute(plain, "wide", [(i, i ^ PAIR) for i in range(owners)])
    sent = spread(plain, partner, owners // 2)
    vecs, live, sent = decode(slot_centroid, lengths, slot_codes, codebook, centroids, sent)
    groups = [[i + z for i in range(owners) if not i & PAIR] for z in (0, PAIR)]
    gathered = lax.all_to_all(
        sent, "wide", split_axis=0, concat_axis=0, axis_index_groups=groups, tiled=True
    ).reshape(tokens, feature)

    core = [(i, i ^ 1) for i in range(4)]
    other = lax.ppermute(vecs, "grp", core)
    far = lax.ppermute(vecs, "grp", [(i, i ^ 2) for i in range(4)])
    far_other = lax.ppermute(far, "grp", core)
    best_shape = jax.ShapeDtypeStruct((passages, tokens), jnp.float32)
    block = pltpu.VMEM((rows, feature), jnp.bfloat16)
    best = pl.pallas_call(
        near_kernel,
        out_shape=best_shape,
        in_specs=[VMEM] * 4,
        out_specs=VMEM,
        scratch_shapes=[pltpu.VMEM((2 * rows, feature), jnp.bfloat16)],
        compiler_params=params(24),
        cost_estimate=cost(tokens, 2 * rows, feature),
        name="score_near",
    )(live, gathered, vecs, other)
    best = pl.pallas_call(
        far_kernel,
        out_shape=best_shape,
        in_specs=[VMEM] * 4,
        out_specs=VMEM,
        scratch_shapes=[block],
        compiler_params=params(24),
        cost_estimate=cost(tokens, rows, feature),
        name="score_far",
    )(live, gathered, far, best)
    table = pl.pallas_call(
        last_kernel,
        out_shape=jax.ShapeDtypeStruct((owners, LANES), jnp.float32),
        in_specs=[VMEM] * 5,
        out_specs=VMEM,
        scratch_shapes=[block, pltpu.VMEM((3 * passages, tokens), jnp.bfloat16)],
        compiler_params=params(24),
        cost_estimate=cost(tokens, rows, feature),
        name="score_last",
    )(live, gathered, far_other, best, members)
    owned = lax.all_to_all(table, "wide", split_axis=0, concat_axis=0, tiled=True)
    return pick(owned, candidates, passages)


def pick_kernel(passages, owned_ref, candidates_ref, out_ref):
    owners = owned_ref.shape[0]
    count, wanted = candidates_ref.shape
    rows = lax.broadcasted_iota(jnp.int32, (owners, LANES), 0)
    held = owned_ref[...]
    for q in range(count):
        for c in range(0, wanted, LANES):
            ids = candidates_ref[q : q + 1, c : c + LANES]
            lane = jnp.broadcast_to(q * passages + ids % passages, (owners, LANES))
            part = jnp.broadcast_to(ids // passages, (owners, LANES))
            found = jnp.take_along_axis(held, lane, axis=1)
            out_ref[q : q + 1, c : c + LANES] = jnp.sum(
                jnp.where(rows == part, found, 0.0), axis=0, keepdims=True
            )


def pick(owned, candidates, passages):
    return pl.pallas_call(
        functools.partial(pick_kernel, passages),
        out_shape=jax.ShapeDtypeStruct(candidates.shape, jnp.float32),
        in_specs=[VMEM, VMEM],
        out_specs=VMEM,
        compiler_params=params(2),
        cost_estimate=pl.CostEstimate(
            flops=candidates.size * owned.shape[0] * 2, bytes_accessed=owned.size * 4, transcendentals=0
        ),
        name="pick",
    )(owned, candidates)


def solution(mesh):
    placed = (
        P(("grp", "wide"), None, None),
        P("grp", None),
        P(),
        P("wide", "grp"),
        P("wide", "grp"),
        P("wide"),
        P(("grp", "wide"), None),
    )
    return jax.shard_map(
        shards, mesh=mesh, in_specs=placed, out_specs=P(("grp", "wide"), None), check_vma=False
    )
```

```python
import functools

import jax
import jax.numpy as jnp
from jax import lax
from jax.experimental import pallas as pl
from jax.experimental.pallas import tpu as pltpu
from jax.sharding import PartitionSpec as P

SLAB = 16
LANES = 128
PER_TILE = 4
PIECES = 4
LOWEST = -1e30
PAIR = 4
NT = (((1,), (1,)), ((), ()))
VMEM = pl.BlockSpec(memory_space=pltpu.VMEM)
ANY = pl.BlockSpec(memory_space=pl.ANY)


def unit(values):
    scale = lax.rsqrt(jnp.sum(values * values, axis=-1, keepdims=True) + 1e-06)
    return (values * scale).astype(jnp.bfloat16)


def members_kernel(query_len, out_ref):
    own, owners, count = out_ref.shape
    query = lax.broadcasted_iota(jnp.int32, (owners, count), 1) // query_len
    owner = lax.broadcasted_iota(jnp.int32, (owners, count), 0)
    pair = (owner // (2 * PAIR)) * PAIR + owner % PAIR
    place = pair * 2 + (owner // PAIR) % 2
    for q in range(own):
        out_ref[q] = (query == place * own + q).astype(jnp.float32).astype(jnp.bfloat16)


def members_of(own, owners, query_len):
    return pl.pallas_call(
        functools.partial(members_kernel, query_len),
        out_shape=jax.ShapeDtypeStruct((own, owners, owners * own * query_len), jnp.bfloat16),
        out_specs=VMEM,
        compiler_params=params(2),
        cost_estimate=pl.CostEstimate(flops=20000000000, bytes_accessed=1000, transcendentals=0),
        name="members",
    )()


def spread_kernel(queries_ref, partner_ref, out_ref):
    rows = queries_ref.shape[0]
    low = (lax.axis_index("wide") & PAIR) == 0
    own = unit(queries_ref[...].astype(jnp.float32))
    partner = unit(partner_ref[...].astype(jnp.float32))
    first, second = jnp.where(low, own, partner), jnp.where(low, partner, own)
    for i in range(out_ref.shape[0]):
        out_ref[i, 0:rows, :] = first
        out_ref[i, rows : 2 * rows, :] = second


def spread(queries, partner, count):
    rows, feature = queries.shape
    return pl.pallas_call(
        spread_kernel,
        out_shape=jax.ShapeDtypeStruct((count, 2 * rows, feature), queries.dtype),
        in_specs=[VMEM, VMEM],
        out_specs=VMEM,
        compiler_params=params(4),
        cost_estimate=pl.CostEstimate(flops=0, bytes_accessed=count * rows * feature * 4, transcendentals=0),
        name="spread",
    )(queries, partner)


def residual_rows(codes, codebook, store):
    tiles = codes.shape[1] // LANES
    table = codebook.astype(jnp.float32)
    low, high = table[:LANES].T, table[LANES:].T
    codes = codes.astype(jnp.float32).astype(jnp.bfloat16)
    stacked = jnp.concatenate(
        [codes[:, c * LANES : (c + 1) * LANES] for c in range(tiles)], axis=0
    )
    feature = lax.broadcasted_iota(jnp.int32, (LANES, LANES), 0)
    lane = lax.broadcasted_iota(jnp.int32, (LANES, LANES), 1)
    for jj in range(PER_TILE):
        pattern = (lane == jj * 32 + feature // 4).astype(jnp.float32).astype(jnp.bfloat16)
        index = lax.dot_general(pattern, stacked, NT, preferred_element_type=jnp.float32)
        index = index.astype(jnp.int32)
        within = index & (LANES - 1)
        parts = []
        for s in range(0, LANES, 8):
            w = within[s : s + 8]
            first = jnp.take_along_axis(low[s : s + 8], w, axis=1)
            second = jnp.take_along_axis(high[s : s + 8], w, axis=1)
            parts.append(jnp.where(index[s : s + 8] < LANES, first, second))
        store(jj, jnp.concatenate(parts, axis=0).T)


def residual_kernel(codes, book, lengths, out, live):
    def store(jj, rows):
        out[jj * LANES : (jj + 1) * LANES, :] = rows

    residual_rows(codes[...], book[...], store)
    count = live.shape[0]
    row = lax.broadcasted_iota(jnp.int32, (count, count), 0)
    lane = lax.broadcasted_iota(jnp.int32, (count, count), 1)
    held = jnp.where(row == lane, jnp.broadcast_to(lengths[...], (count, count)), 0)
    live[...] = jnp.broadcast_to(jnp.sum(held, axis=1, keepdims=True), live.shape)


def gather_kernel(ids, residual, table, out_ref):
    passages, slots = ids.shape
    tiles = slots // PER_TILE
    count = table.shape[0]
    span = passages * SLAB
    row = lax.broadcasted_iota(jnp.int32, (SLAB, LANES), 0)
    fold = (
        lax.broadcasted_iota(jnp.int32, (passages, span), 0)
        == lax.broadcasted_iota(jnp.int32, (passages, span), 1) // SLAB
    ).astype(jnp.float32).astype(jnp.bfloat16)
    for m in range(slots):
        j = (m % tiles) * PER_TILE + m // tiles
        kept = []
        for p in range(passages):
            local = ids[p, j] & (count - 1)
            base = pl.multiple_of(local & ~(SLAB - 1), SLAB)
            slab = table[pl.ds(base, SLAB), :].astype(jnp.float32)
            kept.append(jnp.where(row == (local & (SLAB - 1)), slab, 0.0).astype(jnp.bfloat16))
        centre = jnp.dot(fold, jnp.concatenate(kept, axis=0), preferred_element_type=jnp.float32)
        at = m * passages
        out_ref[at : at + passages, :] = unit(centre + residual[at : at + passages, :])


def decode(slot_centroid, lengths, slot_codes, codebook, centroids, sent):
    passages, slots = slot_centroid.shape
    rows, feature = passages * slots, codebook.shape[1]
    smem = pl.BlockSpec(memory_space=pltpu.SMEM)
    residual, live = pl.pallas_call(
        residual_kernel,
        out_shape=(
            jax.ShapeDtypeStruct((rows, feature), jnp.float32),
            jax.ShapeDtypeStruct((passages, LANES), jnp.int32),
        ),
        in_specs=[VMEM] * 3,
        out_specs=(VMEM, VMEM),
        compiler_params=params(4),
        cost_estimate=pl.CostEstimate(flops=rows * 256 * feature, bytes_accessed=rows * 256, transcendentals=0),
        name="residual",
    )(slot_codes, codebook, lengths.reshape(1, passages))
    residual, sent = lax.optimization_barrier((residual, sent))
    vecs = pl.pallas_call(
        gather_kernel,
        out_shape=jax.ShapeDtypeStruct((rows, feature), jnp.bfloat16),
        in_specs=[smem, VMEM, VMEM],
        out_specs=VMEM,
        compiler_params=params(4 + centroids.size * 2 // (1 << 20)),
        cost_estimate=pl.CostEstimate(
            flops=rows * feature * 8, bytes_accessed=centroids.size * 2, transcendentals=rows
        ),
        name="gather",
    )(slot_centroid, residual, centroids)
    vecs, sent = lax.optimization_barrier((vecs, sent))
    return vecs, live, sent


def maxima(live, tokens, blocks, scratch, store):
    passages = live.shape[0]
    rows = scratch.shape[0] // len(blocks)
    slots = rows // passages
    tiles = slots // PER_TILE
    for b, (begin, vecs) in enumerate(blocks):
        first = vecs[0:passages, :]
        for m in range(slots):
            j = (m % tiles) * PER_TILE + m // tiles
            held = vecs[m * passages : (m + 1) * passages, :]
            if j:
                held = jnp.where(live > begin + j, held, first)
            at = b * rows + m * passages
            scratch[at : at + passages, :] = held

    chunk, span = 1024, 128
    for k in range(0, tokens.shape[0], chunk):
        wanted = tokens[k : k + chunk, :]
        best = None
        for b, (begin, _) in enumerate(blocks):
            top = None
            for s in range(b * rows, (b + 1) * rows, span):
                similar = lax.dot_general(
                    scratch[s : s + span, :], wanted, NT, preferred_element_type=jnp.float32
                )
                here = jnp.max(similar.reshape(span // passages, passages, chunk), axis=0)
                top = here if top is None else jnp.maximum(top, here)
            top = jnp.where(live[:, :1] > begin, top, LOWEST)
            best = top if best is None else jnp.maximum(best, top)
        store(k, best)


def begins(slots):
    own = lax.axis_index("grp")
    return [jnp.bitwise_xor(own, s) * slots for s in range(4)]


def near_kernel(live, tokens, own, other, best_out, scratch):
    begin = begins(own.shape[0] // live.shape[0])

    def store(k, best):
        best_out[:, k : k + best.shape[1]] = best

    maxima(live[...], tokens, [(begin[0], own), (begin[1], other)], scratch, store)


def far_kernel(live, tokens, vecs, before, best_out, scratch):
    begin = begins(vecs.shape[0] // live.shape[0])

    def store(k, best):
        best_out[:, k : k + best.shape[1]] = jnp.maximum(best, before[:, k : k + best.shape[1]])

    maxima(live[...], tokens, [(begin[2], vecs)], scratch, store)


def last_kernel(live, tokens, vecs, before, members, out_ref, scratch, whole):
    passages = live.shape[0]
    begin = begins(vecs.shape[0] // passages)

    def store(k, best):
        best = jnp.maximum(best, before[:, k : k + best.shape[1]])
        high = best.astype(jnp.bfloat16)
        rest = best - high.astype(jnp.float32)
        mid = rest.astype(jnp.bfloat16)
        low = (rest - mid.astype(jnp.float32)).astype(jnp.bfloat16)
        for i, part in enumerate((high, mid, low)):
            whole[i * passages : (i + 1) * passages, k : k + best.shape[1]] = part

    maxima(live[...], tokens, [(begin[3], vecs)], scratch, store)
    for q in range(members.shape[0]):
        sums = lax.dot_general(members[q], whole[...], NT, preferred_element_type=jnp.float32)
        total = sums[:, 2 * passages : 3 * passages] + sums[:, passages : 2 * passages]
        out_ref[:, q * passages : (q + 1) * passages] = total + sums[:, :passages]


def params(mebibytes):
    return pltpu.CompilerParams(vmem_limit_bytes=mebibytes << 20)


def cost(tokens, rows, feature):
    return pl.CostEstimate(
        flops=2 * tokens * rows * feature,
        bytes_accessed=(tokens + rows) * feature * 2,
        transcendentals=tokens,
    )


def shards(queries, centroids, codebook, slot_codes, slot_centroid, lengths, candidates):
    own, query_len, feature = queries.shape
    owners = lax.axis_size("wide")
    passages = lengths.shape[0]
    tokens = owners * own * query_len
    rows = slot_centroid.size
    plain = queries.reshape(own * query_len, feature)
    members = members_of(own, owners, query_len)
    members, slot_codes = lax.optimization_barrier((members, slot_codes))
    partner = lax.ppermute(plain, "wide", [(i, i ^ PAIR) for i in range(owners)])
    sent = spread(plain, partner, owners // 2)
    vecs, live, sent = decode(slot_centroid, lengths, slot_codes, codebook, centroids, sent)
    groups = [[i + z for i in range(owners) if not i & PAIR] for z in (0, PAIR)]
    gathered = lax.all_to_all(
        sent, "wide", split_axis=0, concat_axis=0, axis_index_groups=groups, tiled=True
    ).reshape(tokens, feature)

    core = [(i, i ^ 1) for i in range(4)]
    other = lax.ppermute(vecs, "grp", core)
    far = lax.ppermute(vecs, "grp", [(i, i ^ 2) for i in range(4)])
    far_other = lax.ppermute(far, "grp", core)
    best_shape = jax.ShapeDtypeStruct((passages, tokens), jnp.float32)
    block = pltpu.VMEM((rows, feature), jnp.bfloat16)
    best = pl.pallas_call(
        near_kernel,
        out_shape=best_shape,
        in_specs=[VMEM] * 4,
        out_specs=VMEM,
        scratch_shapes=[pltpu.VMEM((2 * rows, feature), jnp.bfloat16)],
        compiler_params=params(24),
        cost_estimate=cost(tokens, 2 * rows, feature),
        name="score_near",
    )(live, gathered, vecs, other)
    best = pl.pallas_call(
        far_kernel,
        out_shape=best_shape,
        in_specs=[VMEM] * 4,
        out_specs=VMEM,
        scratch_shapes=[block],
        compiler_params=params(24),
        cost_estimate=cost(tokens, rows, feature),
        name="score_far",
    )(live, gathered, far, best)
    table = pl.pallas_call(
        last_kernel,
        out_shape=jax.ShapeDtypeStruct((owners, LANES), jnp.float32),
        in_specs=[VMEM] * 5,
        out_specs=VMEM,
        scratch_shapes=[block, pltpu.VMEM((3 * passages, tokens), jnp.bfloat16)],
        compiler_params=params(24),
        cost_estimate=cost(tokens, rows, feature),
        name="score_last",
    )(live, gathered, far_other, best, members)
    owned = lax.all_to_all(table, "wide", split_axis=0, concat_axis=0, tiled=True)
    return pick(owned, candidates, passages)


def pick_kernel(passages, owned_ref, candidates_ref, out_ref):
    owners = owned_ref.shape[0]
    count, wanted = candidates_ref.shape
    rows = lax.broadcasted_iota(jnp.int32, (owners, LANES), 0)
    held = owned_ref[...]
    for q in range(count):
        for c in range(0, wanted, LANES):
            ids = candidates_ref[q : q + 1, c : c + LANES]
            lane = jnp.broadcast_to(q * passages + ids % passages, (owners, LANES))
            part = jnp.broadcast_to(ids // passages, (owners, LANES))
            found = jnp.take_along_axis(held, lane, axis=1)
            out_ref[q : q + 1, c : c + LANES] = jnp.sum(
                jnp.where(rows == part, found, 0.0), axis=0, keepdims=True
            )


def pick(owned, candidates, passages):
    return pl.pallas_call(
        functools.partial(pick_kernel, passages),
        out_shape=jax.ShapeDtypeStruct(candidates.shape, jnp.float32),
        in_specs=[VMEM, VMEM],
        out_specs=VMEM,
        compiler_params=params(2),
        cost_estimate=pl.CostEstimate(
            flops=candidates.size * owned.shape[0] * 2, bytes_accessed=owned.size * 4, transcendentals=0
        ),
        name="pick",
    )(owned, candidates)


def solution(mesh):
    placed = (
        P(("grp", "wide"), None, None),
        P("grp", None),
        P(),
        P("wide", "grp"),
        P("wide", "grp"),
        P("wide"),
        P(("grp", "wide"), None),
    )
    return jax.shard_map(
        shards, mesh=mesh, in_specs=placed, out_specs=P(("grp", "wide"), None), check_vma=False
    )
```

```python
import functools

import jax
import jax.numpy as jnp
from jax import lax
from jax.experimental import pallas as pl
from jax.experimental.pallas import tpu as pltpu
from jax.sharding import PartitionSpec as P

SLAB = 16
LANES = 128
PER_TILE = 4
PIECES = 4
LOWEST = -1e30
PAIR = 4
TURN = 3
UPPER = 2
NT = (((1,), (1,)), ((), ()))
VMEM = pl.BlockSpec(memory_space=pltpu.VMEM)
ANY = pl.BlockSpec(memory_space=pl.ANY)


def unit(values):
    scale = lax.rsqrt(jnp.sum(values * values, axis=-1, keepdims=True) + 1e-06)
    return (values * scale).astype(jnp.bfloat16)


def members_kernel(query_len, owners, out_ref):
    rows, count = out_ref.shape
    query = lax.broadcasted_iota(jnp.int32, (owners, count), 1) // query_len
    owner = lax.broadcasted_iota(jnp.int32, (owners, count), 0)
    upper = (owner & UPPER) // UPPER
    lower = jnp.where(upper == 1, owner ^ TURN, owner)
    place = ((owner // 8) * 2 + (lower & 1)) * 4 + ((owner & PAIR) // PAIR) * 2 + upper
    own = rows // owners
    for q in range(own):
        here = (query == place * own + q).astype(jnp.float32).astype(jnp.bfloat16)
        out_ref[q * owners : (q + 1) * owners, :] = here


def members_of(own, owners, query_len):
    return pl.pallas_call(
        functools.partial(members_kernel, query_len, owners),
        out_shape=jax.ShapeDtypeStruct((own * owners, owners * own * query_len), jnp.bfloat16),
        out_specs=VMEM,
        compiler_params=params(2),
        cost_estimate=pl.CostEstimate(flops=20000000000, bytes_accessed=1000, transcendentals=0),
        name="members",
    )()


def spread_kernel(own_ref, turned_ref, paired_ref, both_ref, after_ref, out_ref):
    rows = own_ref.shape[0]
    index = lax.axis_index("wide")
    at = ((index & PAIR) // PAIR) * 2 + (index & UPPER) // UPPER
    held = [unit(ref[...].astype(jnp.float32)) for ref in (own_ref, turned_ref, paired_ref, both_ref)]
    for place in range(4):
        step = jnp.bitwise_xor(at, place)
        value = held[3]
        for i in range(3):
            value = jnp.where(step == i, held[i], value)
        for i in range(out_ref.shape[0]):
            out_ref[i, place * rows : (place + 1) * rows, :] = value


def spread(pieces, after, count):
    rows, feature = pieces[0].shape
    return pl.pallas_call(
        spread_kernel,
        out_shape=jax.ShapeDtypeStruct((count, 4 * rows, feature), pieces[0].dtype),
        in_specs=[VMEM] * 4 + [ANY],
        out_specs=VMEM,
        compiler_params=params(4),
        cost_estimate=pl.CostEstimate(flops=0, bytes_accessed=count * rows * feature * 8, transcendentals=0),
        name="spread",
    )(*pieces, after)


def residual_rows(codes, codebook, store):
    tiles = codes.shape[1] // LANES
    table = codebook.astype(jnp.float32)
    low, high = table[:LANES].T, table[LANES:].T
    codes = codes.astype(jnp.float32).astype(jnp.bfloat16)
    stacked = jnp.concatenate(
        [codes[:, c * LANES : (c + 1) * LANES] for c in range(tiles)], axis=0
    )
    feature = lax.broadcasted_iota(jnp.int32, (LANES, LANES), 0)
    lane = lax.broadcasted_iota(jnp.int32, (LANES, LANES), 1)
    for jj in range(PER_TILE):
        pattern = (lane == jj * 32 + feature // 4).astype(jnp.float32).astype(jnp.bfloat16)
        index = lax.dot_general(pattern, stacked, NT, preferred_element_type=jnp.float32)
        index = index.astype(jnp.int32)
        within = index & (LANES - 1)
        parts = []
        for s in range(0, LANES, 8):
            w = within[s : s + 8]
            first = jnp.take_along_axis(low[s : s + 8], w, axis=1)
            second = jnp.take_along_axis(high[s : s + 8], w, axis=1)
            parts.append(jnp.where(index[s : s + 8] < LANES, first, second))
        store(jj, jnp.concatenate(parts, axis=0).T)


def residual_kernel(codes, book, lengths, out, live):
    def store(jj, rows):
        out[jj * LANES : (jj + 1) * LANES, :] = rows

    residual_rows(codes[...], book[...], store)
    count = live.shape[0]
    row = lax.broadcasted_iota(jnp.int32, (count, count), 0)
    lane = lax.broadcasted_iota(jnp.int32, (count, count), 1)
    held = jnp.where(row == lane, jnp.broadcast_to(lengths[...], (count, count)), 0)
    live[...] = jnp.broadcast_to(jnp.sum(held, axis=1, keepdims=True), live.shape)


def gather_kernel(ids, residual, table, out_ref):
    passages, slots = ids.shape
    tiles = slots // PER_TILE
    count = table.shape[0]
    span = passages * SLAB
    row = lax.broadcasted_iota(jnp.int32, (SLAB, LANES), 0)
    fold = (
        lax.broadcasted_iota(jnp.int32, (passages, span), 0)
        == lax.broadcasted_iota(jnp.int32, (passages, span), 1) // SLAB
    ).astype(jnp.float32).astype(jnp.bfloat16)
    for m in range(slots):
        j = (m % tiles) * PER_TILE + m // tiles
        kept = []
        for p in range(passages):
            local = ids[p, j] & (count - 1)
            base = pl.multiple_of(local & ~(SLAB - 1), SLAB)
            slab = table[pl.ds(base, SLAB), :].astype(jnp.float32)
            kept.append(jnp.where(row == (local & (SLAB - 1)), slab, 0.0).astype(jnp.bfloat16))
        centre = jnp.dot(fold, jnp.concatenate(kept, axis=0), preferred_element_type=jnp.float32)
        at = m * passages
        out_ref[at : at + passages, :] = unit(centre + residual[at : at + passages, :])


def decode(slot_centroid, lengths, slot_codes, codebook, centroids):
    passages, slots = slot_centroid.shape
    rows, feature = passages * slots, codebook.shape[1]
    smem = pl.BlockSpec(memory_space=pltpu.SMEM)
    residual, live = pl.pallas_call(
        residual_kernel,
        out_shape=(
            jax.ShapeDtypeStruct((rows, feature), jnp.float32),
            jax.ShapeDtypeStruct((passages, LANES), jnp.int32),
        ),
        in_specs=[VMEM] * 3,
        out_specs=(VMEM, VMEM),
        compiler_params=params(4),
        cost_estimate=pl.CostEstimate(flops=rows * 256 * feature, bytes_accessed=rows * 256, transcendentals=0),
        name="residual",
    )(slot_codes, codebook, lengths.reshape(1, passages))
    vecs = pl.pallas_call(
        gather_kernel,
        out_shape=jax.ShapeDtypeStruct((rows, feature), jnp.bfloat16),
        in_specs=[smem, VMEM, VMEM],
        out_specs=VMEM,
        compiler_params=params(4 + centroids.size * 2 // (1 << 20)),
        cost_estimate=pl.CostEstimate(
            flops=rows * feature * 8, bytes_accessed=centroids.size * 2, transcendentals=rows
        ),
        name="gather",
    )(slot_centroid, residual, centroids)
    return vecs, live


def maxima(live, tokens, blocks, scratch, store):
    passages = live.shape[0]
    rows = scratch.shape[0] // len(blocks)
    slots = rows // passages
    tiles = slots // PER_TILE
    for b, (begin, vecs) in enumerate(blocks):
        first = vecs[0:passages, :]
        for m in range(slots):
            j = (m % tiles) * PER_TILE + m // tiles
            held = vecs[m * passages : (m + 1) * passages, :]
            if j:
                held = jnp.where(live > begin + j, held, first)
            at = b * rows + m * passages
            scratch[at : at + passages, :] = held

    chunk, span = 1024, 128
    for k in range(0, tokens.shape[0], chunk):
        wanted = tokens[k : k + chunk, :]
        best = None
        for b, (begin, _) in enumerate(blocks):
            top = None
            for s in range(b * rows, (b + 1) * rows, span):
                similar = lax.dot_general(
                    scratch[s : s + span, :], wanted, NT, preferred_element_type=jnp.float32
                )
                here = jnp.max(similar.reshape(span // passages, passages, chunk), axis=0)
                top = here if top is None else jnp.maximum(top, here)
            top = jnp.where(live[:, :1] > begin, top, LOWEST)
            best = top if best is None else jnp.maximum(best, top)
        store(k, best)


def begins(slots):
    own = lax.axis_index("grp")
    return [jnp.bitwise_xor(own, s) * slots for s in range(4)]


def near_kernel(live, tokens, own, other, best_out, scratch):
    begin = begins(own.shape[0] // live.shape[0])

    def store(k, best):
        best_out[:, k : k + best.shape[1]] = best

    maxima(live[...], tokens, [(begin[0], own), (begin[1], other)], scratch, store)


def far_kernel(live, tokens, vecs, before, best_out, scratch):
    begin = begins(vecs.shape[0] // live.shape[0])

    def store(k, best):
        best_out[:, k : k + best.shape[1]] = jnp.maximum(best, before[:, k : k + best.shape[1]])

    maxima(live[...], tokens, [(begin[2], vecs)], scratch, store)


def last_kernel(live, tokens, vecs, before, members, out_ref, scratch, whole):
    passages = live.shape[0]
    begin = begins(vecs.shape[0] // passages)

    def store(k, best):
        best = jnp.maximum(best, before[:, k : k + best.shape[1]])
        high = best.astype(jnp.bfloat16)
        rest = best - high.astype(jnp.float32)
        mid = rest.astype(jnp.bfloat16)
        low = (rest - mid.astype(jnp.float32)).astype(jnp.bfloat16)
        for i, part in enumerate((high, mid, low)):
            whole[i * passages : (i + 1) * passages, k : k + best.shape[1]] = part

    maxima(live[...], tokens, [(begin[3], vecs)], scratch, store)
    sums = lax.dot_general(members[...], whole[...], NT, preferred_element_type=jnp.float32)
    total = sums[:, 2 * passages : 3 * passages] + sums[:, passages : 2 * passages]
    total = total + sums[:, :passages]
    owners = out_ref.shape[0]
    for q in range(members.shape[0] // owners):
        out_ref[:, q * passages : (q + 1) * passages] = total[q * owners : (q + 1) * owners]


def params(mebibytes):
    return pltpu.CompilerParams(vmem_limit_bytes=mebibytes << 20)


def cost(tokens, rows, feature):
    return pl.CostEstimate(
        flops=2 * tokens * rows * feature,
        bytes_accessed=(tokens + rows) * feature * 2,
        transcendentals=tokens,
    )


def shards(queries, centroids, codebook, slot_codes, slot_centroid, lengths, candidates):
    own, query_len, feature = queries.shape
    owners = lax.axis_size("wide")
    passages = lengths.shape[0]
    tokens = owners * own * query_len
    rows = slot_centroid.size
    plain = queries.reshape(own * query_len, feature)
    members = members_of(own, owners, query_len)
    members, slot_codes = lax.optimization_barrier((members, slot_codes))
    pieces = [plain] + [
        lax.ppermute(plain, "wide", [(i, i ^ step) for i in range(owners)])
        for step in (TURN, PAIR, TURN ^ PAIR)
    ]
    vecs, live = decode(slot_centroid, lengths, slot_codes, codebook, centroids)
    sent = spread(pieces, vecs, owners // 4)
    base = [i for i in range(owners) if not i & (PAIR | UPPER)]
    groups = [[i ^ step for i in base] for step in (0, TURN, PAIR, TURN ^ PAIR)]
    gathered = lax.all_to_all(
        sent, "wide", split_axis=0, concat_axis=0, axis_index_groups=groups, tiled=True
    ).reshape(tokens, feature)

    core = [(i, i ^ 1) for i in range(4)]
    other = lax.ppermute(vecs, "grp", core)
    far = lax.ppermute(vecs, "grp", [(i, i ^ 2) for i in range(4)])
    far_other = lax.ppermute(far, "grp", core)
    best_shape = jax.ShapeDtypeStruct((passages, tokens), jnp.float32)
    block = pltpu.VMEM((rows, feature), jnp.bfloat16)
    best = pl.pallas_call(
        near_kernel,
        out_shape=best_shape,
        in_specs=[VMEM] * 4,
        out_specs=VMEM,
        scratch_shapes=[pltpu.VMEM((2 * rows, feature), jnp.bfloat16)],
        compiler_params=params(24),
        cost_estimate=cost(tokens, 2 * rows, feature),
        name="score_near",
    )(live, gathered, vecs, other)
    best = pl.pallas_call(
        far_kernel,
        out_shape=best_shape,
        in_specs=[VMEM] * 4,
        out_specs=VMEM,
        scratch_shapes=[block],
        compiler_params=params(24),
        cost_estimate=cost(tokens, rows, feature),
        name="score_far",
    )(live, gathered, far, best)
    table = pl.pallas_call(
        last_kernel,
        out_shape=jax.ShapeDtypeStruct((owners, LANES), jnp.float32),
        in_specs=[VMEM] * 5,
        out_specs=VMEM,
        scratch_shapes=[block, pltpu.VMEM((3 * passages, tokens), jnp.bfloat16)],
        compiler_params=params(24),
        cost_estimate=cost(tokens, rows, feature),
        name="score_last",
    )(live, gathered, far_other, best, members)
    owned = lax.all_to_all(table, "wide", split_axis=0, concat_axis=0, tiled=True)
    return pick(owned, candidates, passages)


def pick_kernel(passages, owned_ref, candidates_ref, out_ref):
    owners = owned_ref.shape[0]
    count, wanted = candidates_ref.shape
    rows = lax.broadcasted_iota(jnp.int32, (owners, LANES), 0)
    held = owned_ref[...]
    for q in range(count):
        for c in range(0, wanted, LANES):
            ids = candidates_ref[q : q + 1, c : c + LANES]
            lane = jnp.broadcast_to(q * passages + ids % passages, (owners, LANES))
            part = jnp.broadcast_to(ids // passages, (owners, LANES))
            found = jnp.take_along_axis(held, lane, axis=1)
            out_ref[q : q + 1, c : c + LANES] = jnp.sum(
                jnp.where(rows == part, found, 0.0), axis=0, keepdims=True
            )


def pick(owned, candidates, passages):
    return pl.pallas_call(
        functools.partial(pick_kernel, passages),
        out_shape=jax.ShapeDtypeStruct(candidates.shape, jnp.float32),
        in_specs=[VMEM, VMEM],
        out_specs=VMEM,
        compiler_params=params(2),
        cost_estimate=pl.CostEstimate(
            flops=candidates.size * owned.shape[0] * 2, bytes_accessed=owned.size * 4, transcendentals=0
        ),
        name="pick",
    )(owned, candidates)


def solution(mesh):
    placed = (
        P(("grp", "wide"), None, None),
        P("grp", None),
        P(),
        P("wide", "grp"),
        P("wide", "grp"),
        P("wide"),
        P(("grp", "wide"), None),
    )
    return jax.shard_map(
        shards, mesh=mesh, in_specs=placed, out_specs=P(("grp", "wide"), None), check_vma=False
    )
```

```python
import functools

import jax
import jax.numpy as jnp
from jax import lax
from jax.experimental import pallas as pl
from jax.experimental.pallas import tpu as pltpu
from jax.sharding import PartitionSpec as P

SLAB = 16
LANES = 128
PER_TILE = 4
PIECES = 4
LOWEST = -1e30
PAIR = 4
TURN = 3
UPPER = 2
NT = (((1,), (1,)), ((), ()))
VMEM = pl.BlockSpec(memory_space=pltpu.VMEM)
ANY = pl.BlockSpec(memory_space=pl.ANY)


def unit(values):
    scale = lax.rsqrt(jnp.sum(values * values, axis=-1, keepdims=True) + 1e-06)
    return (values * scale).astype(jnp.bfloat16)


def members_kernel(query_len, owners, out_ref):
    rows, count = out_ref.shape
    query = lax.broadcasted_iota(jnp.int32, (owners, count), 1) // query_len
    owner = lax.broadcasted_iota(jnp.int32, (owners, count), 0)
    upper = (owner & UPPER) // UPPER
    lower = jnp.where(upper == 1, owner ^ TURN, owner)
    place = ((owner // 8) * 2 + (lower & 1)) * 4 + ((owner & PAIR) // PAIR) * 2 + upper
    own = rows // owners
    for q in range(own):
        here = (query == place * own + q).astype(jnp.float32).astype(jnp.bfloat16)
        out_ref[q * owners : (q + 1) * owners, :] = here


def members_of(own, owners, query_len):
    return pl.pallas_call(
        functools.partial(members_kernel, query_len, owners),
        out_shape=jax.ShapeDtypeStruct((own * owners, owners * own * query_len), jnp.bfloat16),
        out_specs=VMEM,
        compiler_params=params(2),
        cost_estimate=pl.CostEstimate(flops=20000000000, bytes_accessed=1000, transcendentals=0),
        name="members",
    )()


def spread_kernel(own_ref, turned_ref, paired_ref, both_ref, after_ref, out_ref):
    rows = own_ref.shape[0]
    index = lax.axis_index("wide")
    at = ((index & PAIR) // PAIR) * 2 + (index & UPPER) // UPPER
    held = [unit(ref[...].astype(jnp.float32)) for ref in (own_ref, turned_ref, paired_ref, both_ref)]
    for place in range(4):
        step = jnp.bitwise_xor(at, place)
        value = held[3]
        for i in range(3):
            value = jnp.where(step == i, held[i], value)
        for i in range(out_ref.shape[0]):
            out_ref[i, place * rows : (place + 1) * rows, :] = value


def spread(pieces, after, count):
    rows, feature = pieces[0].shape
    return pl.pallas_call(
        spread_kernel,
        out_shape=jax.ShapeDtypeStruct((count, 4 * rows, feature), pieces[0].dtype),
        in_specs=[VMEM] * 4 + [ANY],
        out_specs=VMEM,
        compiler_params=params(4),
        cost_estimate=pl.CostEstimate(flops=0, bytes_accessed=count * rows * feature * 8, transcendentals=0),
        name="spread",
    )(*pieces, after)


def residual_rows(codes, codebook, store):
    tiles = codes.shape[1] // LANES
    table = codebook.astype(jnp.float32)
    low, high = table[:LANES].T, table[LANES:].T
    codes = codes.astype(jnp.float32).astype(jnp.bfloat16)
    stacked = jnp.concatenate(
        [codes[:, c * LANES : (c + 1) * LANES] for c in range(tiles)], axis=0
    )
    feature = lax.broadcasted_iota(jnp.int32, (LANES, LANES), 0)
    lane = lax.broadcasted_iota(jnp.int32, (LANES, LANES), 1)
    for jj in range(PER_TILE):
        pattern = (lane == jj * 32 + feature // 4).astype(jnp.float32).astype(jnp.bfloat16)
        index = lax.dot_general(pattern, stacked, NT, preferred_element_type=jnp.float32)
        index = index.astype(jnp.int32)
        within = index & (LANES - 1)
        parts = []
        for s in range(0, LANES, 8):
            w = within[s : s + 8]
            first = jnp.take_along_axis(low[s : s + 8], w, axis=1)
            second = jnp.take_along_axis(high[s : s + 8], w, axis=1)
            parts.append(jnp.where(index[s : s + 8] < LANES, first, second))
        store(jj, jnp.concatenate(parts, axis=0).T)


def residual_kernel(codes, book, lengths, out, live):
    def store(jj, rows):
        out[jj * LANES : (jj + 1) * LANES, :] = rows

    residual_rows(codes[...], book[...], store)
    count = live.shape[0]
    row = lax.broadcasted_iota(jnp.int32, (count, count), 0)
    lane = lax.broadcasted_iota(jnp.int32, (count, count), 1)
    held = jnp.where(row == lane, jnp.broadcast_to(lengths[...], (count, count)), 0)
    live[...] = jnp.broadcast_to(jnp.sum(held, axis=1, keepdims=True), live.shape)


def gather_kernel(ids, residual, table, out_ref):
    passages, slots = ids.shape
    tiles = slots // PER_TILE
    count = table.shape[0]
    span = passages * SLAB
    row = lax.broadcasted_iota(jnp.int32, (SLAB, LANES), 0)
    fold = (
        lax.broadcasted_iota(jnp.int32, (passages, span), 0)
        == lax.broadcasted_iota(jnp.int32, (passages, span), 1) // SLAB
    ).astype(jnp.float32).astype(jnp.bfloat16)
    for m in range(slots):
        j = (m % tiles) * PER_TILE + m // tiles
        kept = []
        for p in range(passages):
            local = ids[p, j] & (count - 1)
            base = pl.multiple_of(local & ~(SLAB - 1), SLAB)
            slab = table[pl.ds(base, SLAB), :].astype(jnp.float32)
            kept.append(jnp.where(row == (local & (SLAB - 1)), slab, 0.0).astype(jnp.bfloat16))
        centre = jnp.dot(fold, jnp.concatenate(kept, axis=0), preferred_element_type=jnp.float32)
        at = m * passages
        out_ref[at : at + passages, :] = unit(centre + residual[at : at + passages, :])


def decode(slot_centroid, lengths, slot_codes, codebook, centroids):
    passages, slots = slot_centroid.shape
    rows, feature = passages * slots, codebook.shape[1]
    smem = pl.BlockSpec(memory_space=pltpu.SMEM)
    residual, live = pl.pallas_call(
        residual_kernel,
        out_shape=(
            jax.ShapeDtypeStruct((rows, feature), jnp.float32),
            jax.ShapeDtypeStruct((passages, LANES), jnp.int32),
        ),
        in_specs=[VMEM] * 3,
        out_specs=(VMEM, VMEM),
        compiler_params=params(4),
        cost_estimate=pl.CostEstimate(flops=rows * 256 * feature, bytes_accessed=rows * 256, transcendentals=0),
        name="residual",
    )(slot_codes, codebook, lengths.reshape(1, passages))
    vecs = pl.pallas_call(
        gather_kernel,
        out_shape=jax.ShapeDtypeStruct((rows, feature), jnp.bfloat16),
        in_specs=[smem, VMEM, VMEM],
        out_specs=VMEM,
        compiler_params=params(4 + centroids.size * 2 // (1 << 20)),
        cost_estimate=pl.CostEstimate(
            flops=rows * feature * 8, bytes_accessed=centroids.size * 2, transcendentals=rows
        ),
        name="gather",
    )(slot_centroid, residual, centroids)
    return vecs, live


def maxima(live, tokens, blocks, scratch, store):
    passages = live.shape[0]
    rows = scratch.shape[0] // len(blocks)
    slots = rows // passages
    tiles = slots // PER_TILE
    for b, (begin, vecs) in enumerate(blocks):
        first = vecs[0:passages, :]
        for m in range(slots):
            j = (m % tiles) * PER_TILE + m // tiles
            held = vecs[m * passages : (m + 1) * passages, :]
            if j:
                held = jnp.where(live > begin + j, held, first)
            at = b * rows + m * passages
            scratch[at : at + passages, :] = held

    chunk, span = 1024, 128
    for k in range(0, tokens.shape[0], chunk):
        wanted = tokens[k : k + chunk, :]
        best = None
        for b, (begin, _) in enumerate(blocks):
            top = None
            for s in range(b * rows, (b + 1) * rows, span):
                similar = lax.dot_general(
                    scratch[s : s + span, :], wanted, NT, preferred_element_type=jnp.float32
                )
                here = jnp.max(similar.reshape(span // passages, passages, chunk), axis=0)
                top = here if top is None else jnp.maximum(top, here)
            top = jnp.where(live[:, :1] > begin, top, LOWEST)
            best = top if best is None else jnp.maximum(best, top)
        store(k, best)


def begins(slots):
    own = lax.axis_index("grp")
    return [jnp.bitwise_xor(own, s) * slots for s in range(4)]


def first_kernel(live, tokens, own, other, far, best_out, scratch):
    begin = begins(own.shape[0] // live.shape[0])

    def store(k, best):
        best_out[:, k : k + best.shape[1]] = best

    blocks = list(zip(begin[:3], (own, other, far)))
    maxima(live[...], tokens, blocks, scratch, store)


def last_kernel(live, tokens, vecs, before, members, out_ref, scratch, whole):
    passages = live.shape[0]
    begin = begins(vecs.shape[0] // passages)

    def store(k, best):
        best = jnp.maximum(best, before[:, k : k + best.shape[1]])
        high = best.astype(jnp.bfloat16)
        rest = best - high.astype(jnp.float32)
        mid = rest.astype(jnp.bfloat16)
        low = (rest - mid.astype(jnp.float32)).astype(jnp.bfloat16)
        for i, part in enumerate((high, mid, low)):
            whole[i * passages : (i + 1) * passages, k : k + best.shape[1]] = part

    maxima(live[...], tokens, [(begin[3], vecs)], scratch, store)
    sums = lax.dot_general(members[...], whole[...], NT, preferred_element_type=jnp.float32)
    total = sums[:, 2 * passages : 3 * passages] + sums[:, passages : 2 * passages]
    total = total + sums[:, :passages]
    owners = out_ref.shape[0]
    for q in range(members.shape[0] // owners):
        out_ref[:, q * passages : (q + 1) * passages] = total[q * owners : (q + 1) * owners]


def params(mebibytes):
    return pltpu.CompilerParams(vmem_limit_bytes=mebibytes << 20)


def cost(tokens, rows, feature):
    return pl.CostEstimate(
        flops=2 * tokens * rows * feature,
        bytes_accessed=(tokens + rows) * feature * 2,
        transcendentals=tokens,
    )


def shards(queries, centroids, codebook, slot_codes, slot_centroid, lengths, candidates):
    own, query_len, feature = queries.shape
    owners = lax.axis_size("wide")
    passages = lengths.shape[0]
    tokens = owners * own * query_len
    rows = slot_centroid.size
    plain = queries.reshape(own * query_len, feature)
    members = members_of(own, owners, query_len)
    members, slot_codes = lax.optimization_barrier((members, slot_codes))
    pieces = [plain] + [
        lax.ppermute(plain, "wide", [(i, i ^ step) for i in range(owners)])
        for step in (TURN, PAIR, TURN ^ PAIR)
    ]
    vecs, live = decode(slot_centroid, lengths, slot_codes, codebook, centroids)
    sent = spread(pieces, vecs, owners // 4)
    base = [i for i in range(owners) if not i & (PAIR | UPPER)]
    groups = [[i ^ step for i in base] for step in (0, TURN, PAIR, TURN ^ PAIR)]
    gathered = lax.all_to_all(
        sent, "wide", split_axis=0, concat_axis=0, axis_index_groups=groups, tiled=True
    ).reshape(tokens, feature)

    core = [(i, i ^ 1) for i in range(4)]
    other = lax.ppermute(vecs, "grp", core)
    far = lax.ppermute(vecs, "grp", [(i, i ^ 2) for i in range(4)])
    far_other = lax.ppermute(far, "grp", core)
    best_shape = jax.ShapeDtypeStruct((passages, tokens), jnp.float32)
    block = pltpu.VMEM((rows, feature), jnp.bfloat16)
    best = pl.pallas_call(
        first_kernel,
        out_shape=best_shape,
        in_specs=[VMEM] * 5,
        out_specs=VMEM,
        scratch_shapes=[pltpu.VMEM((3 * rows, feature), jnp.bfloat16)],
        compiler_params=params(24),
        cost_estimate=cost(tokens, 3 * rows, feature),
        name="score_first",
    )(live, gathered, vecs, other, far)
    table = pl.pallas_call(
        last_kernel,
        out_shape=jax.ShapeDtypeStruct((owners, LANES), jnp.float32),
        in_specs=[VMEM] * 5,
        out_specs=VMEM,
        scratch_shapes=[block, pltpu.VMEM((3 * passages, tokens), jnp.bfloat16)],
        compiler_params=params(24),
        cost_estimate=cost(tokens, rows, feature),
        name="score_last",
    )(live, gathered, far_other, best, members)
    owned = lax.all_to_all(table, "wide", split_axis=0, concat_axis=0, tiled=True)
    return pick(owned, candidates, passages)


def pick_kernel(passages, owned_ref, candidates_ref, out_ref):
    owners = owned_ref.shape[0]
    count, wanted = candidates_ref.shape
    rows = lax.broadcasted_iota(jnp.int32, (owners, LANES), 0)
    held = owned_ref[...]
    for q in range(count):
        for c in range(0, wanted, LANES):
            ids = candidates_ref[q : q + 1, c : c + LANES]
            lane = jnp.broadcast_to(q * passages + ids % passages, (owners, LANES))
            part = jnp.broadcast_to(ids // passages, (owners, LANES))
            found = jnp.take_along_axis(held, lane, axis=1)
            out_ref[q : q + 1, c : c + LANES] = jnp.sum(
                jnp.where(rows == part, found, 0.0), axis=0, keepdims=True
            )


def pick(owned, candidates, passages):
    return pl.pallas_call(
        functools.partial(pick_kernel, passages),
        out_shape=jax.ShapeDtypeStruct(candidates.shape, jnp.float32),
        in_specs=[VMEM, VMEM],
        out_specs=VMEM,
        compiler_params=params(2),
        cost_estimate=pl.CostEstimate(
            flops=candidates.size * owned.shape[0] * 2, bytes_accessed=owned.size * 4, transcendentals=0
        ),
        name="pick",
    )(owned, candidates)


def solution(mesh):
    placed = (
        P(("grp", "wide"), None, None),
        P("grp", None),
        P(),
        P("wide", "grp"),
        P("wide", "grp"),
        P("wide"),
        P(("grp", "wide"), None),
    )
    return jax.shard_map(
        shards, mesh=mesh, in_specs=placed, out_specs=P(("grp", "wide"), None), check_vma=False
    )
```

```python
import functools

import jax
import jax.numpy as jnp
from jax import lax
from jax.experimental import pallas as pl
from jax.experimental.pallas import tpu as pltpu
from jax.sharding import PartitionSpec as P

SLAB = 16
LANES = 128
PER_TILE = 4
PIECES = 4
LOWEST = -1e30
PAIR = 4
TURN = 3
UPPER = 2
NT = (((1,), (1,)), ((), ()))
VMEM = pl.BlockSpec(memory_space=pltpu.VMEM)
ANY = pl.BlockSpec(memory_space=pl.ANY)


def unit(values):
    scale = lax.rsqrt(jnp.sum(values * values, axis=-1, keepdims=True) + 1e-06)
    return (values * scale).astype(jnp.bfloat16)


def members_kernel(query_len, owners, out_ref):
    rows, count = out_ref.shape
    query = lax.broadcasted_iota(jnp.int32, (owners, count), 1) // query_len
    owner = lax.broadcasted_iota(jnp.int32, (owners, count), 0)
    upper = (owner & UPPER) // UPPER
    lower = jnp.where(upper == 1, owner ^ TURN, owner)
    place = ((owner // 8) * 2 + (lower & 1)) * 4 + ((owner & PAIR) // PAIR) * 2 + upper
    own = rows // owners
    for q in range(own):
        here = (query == place * own + q).astype(jnp.float32).astype(jnp.bfloat16)
        out_ref[q * owners : (q + 1) * owners, :] = here


def members_of(own, owners, query_len):
    return pl.pallas_call(
        functools.partial(members_kernel, query_len, owners),
        out_shape=jax.ShapeDtypeStruct((own * owners, owners * own * query_len), jnp.bfloat16),
        out_specs=VMEM,
        compiler_params=params(2),
        cost_estimate=pl.CostEstimate(flops=20000000000, bytes_accessed=1000, transcendentals=0),
        name="members",
    )()


def spread_kernel(own_ref, turned_ref, paired_ref, both_ref, after_ref, out_ref):
    rows = own_ref.shape[0]
    index = lax.axis_index("wide")
    at = ((index & PAIR) // PAIR) * 2 + (index & UPPER) // UPPER
    held = [unit(ref[...].astype(jnp.float32)) for ref in (own_ref, turned_ref, paired_ref, both_ref)]
    for place in range(4):
        step = jnp.bitwise_xor(at, place)
        value = held[3]
        for i in range(3):
            value = jnp.where(step == i, held[i], value)
        for i in range(out_ref.shape[0]):
            out_ref[i, place * rows : (place + 1) * rows, :] = value


def spread(pieces, after, count):
    rows, feature = pieces[0].shape
    return pl.pallas_call(
        spread_kernel,
        out_shape=jax.ShapeDtypeStruct((count, 4 * rows, feature), pieces[0].dtype),
        in_specs=[VMEM] * 4 + [ANY],
        out_specs=VMEM,
        compiler_params=params(4),
        cost_estimate=pl.CostEstimate(flops=0, bytes_accessed=count * rows * feature * 8, transcendentals=0),
        name="spread",
    )(*pieces, after)


def residual_rows(codes, codebook, store):
    tiles = codes.shape[1] // LANES
    table = codebook.astype(jnp.float32)
    low, high = table[:LANES].T, table[LANES:].T
    codes = codes.astype(jnp.float32).astype(jnp.bfloat16)
    stacked = jnp.concatenate(
        [codes[:, c * LANES : (c + 1) * LANES] for c in range(tiles)], axis=0
    )
    feature = lax.broadcasted_iota(jnp.int32, (LANES, LANES), 0)
    lane = lax.broadcasted_iota(jnp.int32, (LANES, LANES), 1)
    for jj in range(PER_TILE):
        pattern = (lane == jj * 32 + feature // 4).astype(jnp.float32).astype(jnp.bfloat16)
        index = lax.dot_general(pattern, stacked, NT, preferred_element_type=jnp.float32)
        index = index.astype(jnp.int32)
        within = index & (LANES - 1)
        parts = []
        for s in range(0, LANES, 8):
            w = within[s : s + 8]
            first = jnp.take_along_axis(low[s : s + 8], w, axis=1)
            second = jnp.take_along_axis(high[s : s + 8], w, axis=1)
            parts.append(jnp.where(index[s : s + 8] < LANES, first, second))
        store(jj, jnp.concatenate(parts, axis=0).T)


def residual_kernel(codes, book, lengths, out, live):
    def store(jj, rows):
        out[jj * LANES : (jj + 1) * LANES, :] = rows

    residual_rows(codes[...], book[...], store)
    count = live.shape[0]
    row = lax.broadcasted_iota(jnp.int32, (count, count), 0)
    lane = lax.broadcasted_iota(jnp.int32, (count, count), 1)
    held = jnp.where(row == lane, jnp.broadcast_to(lengths[...], (count, count)), 0)
    live[...] = jnp.broadcast_to(jnp.sum(held, axis=1, keepdims=True), live.shape)


def gather_kernel(ids, residual, table, out_ref):
    passages, slots = ids.shape
    tiles = slots // PER_TILE
    count = table.shape[0]
    span = passages * SLAB
    row = lax.broadcasted_iota(jnp.int32, (SLAB, LANES), 0).astype(jnp.int16)
    none = jnp.zeros((SLAB, LANES), jnp.bfloat16)
    fold = (
        lax.broadcasted_iota(jnp.int32, (passages, span), 0)
        == lax.broadcasted_iota(jnp.int32, (passages, span), 1) // SLAB
    ).astype(jnp.float32).astype(jnp.bfloat16)
    for m in range(slots):
        j = (m % tiles) * PER_TILE + m // tiles
        kept = []
        for p in range(passages):
            local = ids[p, j] & (count - 1)
            base = pl.multiple_of(local & ~(SLAB - 1), SLAB)
            wanted = jnp.full((SLAB, LANES), local & (SLAB - 1), jnp.int32).astype(jnp.int16)
            kept.append(jnp.where(row == wanted, table[pl.ds(base, SLAB), :], none))
        centre = jnp.dot(fold, jnp.concatenate(kept, axis=0), preferred_element_type=jnp.float32)
        at = m * passages
        out_ref[at : at + passages, :] = unit(centre + residual[at : at + passages, :])


def decode(slot_centroid, lengths, slot_codes, codebook, centroids):
    passages, slots = slot_centroid.shape
    rows, feature = passages * slots, codebook.shape[1]
    smem = pl.BlockSpec(memory_space=pltpu.SMEM)
    residual, live = pl.pallas_call(
        residual_kernel,
        out_shape=(
            jax.ShapeDtypeStruct((rows, feature), jnp.float32),
            jax.ShapeDtypeStruct((passages, LANES), jnp.int32),
        ),
        in_specs=[VMEM] * 3,
        out_specs=(VMEM, VMEM),
        compiler_params=params(4),
        cost_estimate=pl.CostEstimate(flops=rows * 256 * feature, bytes_accessed=rows * 256, transcendentals=0),
        name="residual",
    )(slot_codes, codebook, lengths.reshape(1, passages))
    vecs = pl.pallas_call(
        gather_kernel,
        out_shape=jax.ShapeDtypeStruct((rows, feature), jnp.bfloat16),
        in_specs=[smem, VMEM, VMEM],
        out_specs=VMEM,
        compiler_params=params(4 + centroids.size * 2 // (1 << 20)),
        cost_estimate=pl.CostEstimate(
            flops=rows * feature * 8, bytes_accessed=centroids.size * 2, transcendentals=rows
        ),
        name="gather",
    )(slot_centroid, residual, centroids)
    return vecs, live


def maxima(live, tokens, blocks, scratch, store):
    passages = live.shape[0]
    rows = scratch.shape[0] // len(blocks)
    slots = rows // passages
    tiles = slots // PER_TILE
    for b, (begin, vecs) in enumerate(blocks):
        first = vecs[0:passages, :]
        for m in range(slots):
            j = (m % tiles) * PER_TILE + m // tiles
            held = vecs[m * passages : (m + 1) * passages, :]
            if j:
                held = jnp.where(live > begin + j, held, first)
            at = b * rows + m * passages
            scratch[at : at + passages, :] = held

    chunk, span = 1024, 128
    for k in range(0, tokens.shape[0], chunk):
        wanted = tokens[k : k + chunk, :]
        best = None
        for b, (begin, _) in enumerate(blocks):
            top = None
            for s in range(b * rows, (b + 1) * rows, span):
                similar = lax.dot_general(
                    scratch[s : s + span, :], wanted, NT, preferred_element_type=jnp.float32
                )
                here = jnp.max(similar.reshape(span // passages, passages, chunk), axis=0)
                top = here if top is None else jnp.maximum(top, here)
            top = jnp.where(live[:, :1] > begin, top, LOWEST)
            best = top if best is None else jnp.maximum(best, top)
        store(k, best)


def begins(slots):
    own = lax.axis_index("grp")
    return [jnp.bitwise_xor(own, s) * slots for s in range(4)]


def first_kernel(live, tokens, own, other, far, best_out, scratch):
    begin = begins(own.shape[0] // live.shape[0])

    def store(k, best):
        best_out[:, k : k + best.shape[1]] = best

    blocks = list(zip(begin[:3], (own, other, far)))
    maxima(live[...], tokens, blocks, scratch, store)


def last_kernel(live, tokens, vecs, before, members, out_ref, scratch, whole):
    passages = live.shape[0]
    begin = begins(vecs.shape[0] // passages)

    def store(k, best):
        best = jnp.maximum(best, before[:, k : k + best.shape[1]])
        high = best.astype(jnp.bfloat16)
        rest = best - high.astype(jnp.float32)
        mid = rest.astype(jnp.bfloat16)
        low = (rest - mid.astype(jnp.float32)).astype(jnp.bfloat16)
        for i, part in enumerate((high, mid, low)):
            whole[i * passages : (i + 1) * passages, k : k + best.shape[1]] = part

    maxima(live[...], tokens, [(begin[3], vecs)], scratch, store)
    sums = lax.dot_general(members[...], whole[...], NT, preferred_element_type=jnp.float32)
    total = sums[:, 2 * passages : 3 * passages] + sums[:, passages : 2 * passages]
    total = total + sums[:, :passages]
    owners = out_ref.shape[0]
    for q in range(members.shape[0] // owners):
        out_ref[:, q * passages : (q + 1) * passages] = total[q * owners : (q + 1) * owners]


def params(mebibytes):
    return pltpu.CompilerParams(vmem_limit_bytes=mebibytes << 20)


def cost(tokens, rows, feature):
    return pl.CostEstimate(
        flops=2 * tokens * rows * feature,
        bytes_accessed=(tokens + rows) * feature * 2,
        transcendentals=tokens,
    )


def shards(queries, centroids, codebook, slot_codes, slot_centroid, lengths, candidates):
    own, query_len, feature = queries.shape
    owners = lax.axis_size("wide")
    passages = lengths.shape[0]
    tokens = owners * own * query_len
    rows = slot_centroid.size
    plain = queries.reshape(own * query_len, feature)
    members = members_of(own, owners, query_len)
    members, slot_codes = lax.optimization_barrier((members, slot_codes))
    pieces = [plain] + [
        lax.ppermute(plain, "wide", [(i, i ^ step) for i in range(owners)])
        for step in (TURN, PAIR, TURN ^ PAIR)
    ]
    vecs, live = decode(slot_centroid, lengths, slot_codes, codebook, centroids)
    sent = spread(pieces, vecs, owners // 4)
    base = [i for i in range(owners) if not i & (PAIR | UPPER)]
    groups = [[i ^ step for i in base] for step in (0, TURN, PAIR, TURN ^ PAIR)]
    gathered = lax.all_to_all(
        sent, "wide", split_axis=0, concat_axis=0, axis_index_groups=groups, tiled=True
    ).reshape(tokens, feature)

    core = [(i, i ^ 1) for i in range(4)]
    other = lax.ppermute(vecs, "grp", core)
    far = lax.ppermute(vecs, "grp", [(i, i ^ 2) for i in range(4)])
    far_other = lax.ppermute(far, "grp", core)
    best_shape = jax.ShapeDtypeStruct((passages, tokens), jnp.float32)
    block = pltpu.VMEM((rows, feature), jnp.bfloat16)
    best = pl.pallas_call(
        first_kernel,
        out_shape=best_shape,
        in_specs=[VMEM] * 5,
        out_specs=VMEM,
        scratch_shapes=[pltpu.VMEM((3 * rows, feature), jnp.bfloat16)],
        compiler_params=params(24),
        cost_estimate=cost(tokens, 3 * rows, feature),
        name="score_first",
    )(live, gathered, vecs, other, far)
    table = pl.pallas_call(
        last_kernel,
        out_shape=jax.ShapeDtypeStruct((owners, LANES), jnp.float32),
        in_specs=[VMEM] * 5,
        out_specs=VMEM,
        scratch_shapes=[block, pltpu.VMEM((3 * passages, tokens), jnp.bfloat16)],
        compiler_params=params(24),
        cost_estimate=cost(tokens, rows, feature),
        name="score_last",
    )(live, gathered, far_other, best, members)
    owned = lax.all_to_all(table, "wide", split_axis=0, concat_axis=0, tiled=True)
    return pick(owned, candidates, passages)


def pick_kernel(passages, owned_ref, candidates_ref, out_ref):
    owners = owned_ref.shape[0]
    count, wanted = candidates_ref.shape
    rows = lax.broadcasted_iota(jnp.int32, (owners, LANES), 0)
    held = owned_ref[...]
    for q in range(count):
        for c in range(0, wanted, LANES):
            ids = candidates_ref[q : q + 1, c : c + LANES]
            lane = jnp.broadcast_to(q * passages + ids % passages, (owners, LANES))
            part = jnp.broadcast_to(ids // passages, (owners, LANES))
            found = jnp.take_along_axis(held, lane, axis=1)
            out_ref[q : q + 1, c : c + LANES] = jnp.sum(
                jnp.where(rows == part, found, 0.0), axis=0, keepdims=True
            )


def pick(owned, candidates, passages):
    return pl.pallas_call(
        functools.partial(pick_kernel, passages),
        out_shape=jax.ShapeDtypeStruct(candidates.shape, jnp.float32),
        in_specs=[VMEM, VMEM],
        out_specs=VMEM,
        compiler_params=params(2),
        cost_estimate=pl.CostEstimate(
            flops=candidates.size * owned.shape[0] * 2, bytes_accessed=owned.size * 4, transcendentals=0
        ),
        name="pick",
    )(owned, candidates)


def solution(mesh):
    placed = (
        P(("grp", "wide"), None, None),
        P("grp", None),
        P(),
        P("wide", "grp"),
        P("wide", "grp"),
        P("wide"),
        P(("grp", "wide"), None),
    )
    return jax.shard_map(
        shards, mesh=mesh, in_specs=placed, out_specs=P(("grp", "wide"), None), check_vma=False
    )
```

```python
import functools

import jax
import jax.numpy as jnp
from jax import lax
from jax.experimental import pallas as pl
from jax.experimental.pallas import tpu as pltpu
from jax.sharding import PartitionSpec as P

SLAB = 16
LANES = 128
PER_TILE = 4
PIECES = 4
LOWEST = -1e30
PAIR = 4
TURN = 3
UPPER = 2
NT = (((1,), (1,)), ((), ()))
VMEM = pl.BlockSpec(memory_space=pltpu.VMEM)
ANY = pl.BlockSpec(memory_space=pl.ANY)


def unit(values):
    scale = lax.rsqrt(jnp.sum(values * values, axis=-1, keepdims=True) + 1e-06)
    return (values * scale).astype(jnp.bfloat16)


def members_kernel(query_len, owners, out_ref):
    rows, count = out_ref.shape
    query = lax.broadcasted_iota(jnp.int32, (owners, count), 1) // query_len
    owner = lax.broadcasted_iota(jnp.int32, (owners, count), 0)
    upper = (owner & UPPER) // UPPER
    lower = jnp.where(upper == 1, owner ^ TURN, owner)
    place = ((owner // 8) * 2 + (lower & 1)) * 4 + ((owner & PAIR) // PAIR) * 2 + upper
    own = rows // owners
    for q in range(own):
        here = (query == place * own + q).astype(jnp.float32).astype(jnp.bfloat16)
        out_ref[q * owners : (q + 1) * owners, :] = here


def members_of(own, owners, query_len):
    return pl.pallas_call(
        functools.partial(members_kernel, query_len, owners),
        out_shape=jax.ShapeDtypeStruct((own * owners, owners * own * query_len), jnp.bfloat16),
        out_specs=VMEM,
        compiler_params=params(2),
        cost_estimate=pl.CostEstimate(flops=20000000000, bytes_accessed=1000, transcendentals=0),
        name="members",
    )()


def spread_kernel(own_ref, turned_ref, paired_ref, both_ref, after_ref, out_ref):
    rows = own_ref.shape[0]
    index = lax.axis_index("wide")
    at = ((index & PAIR) // PAIR) * 2 + (index & UPPER) // UPPER
    held = [unit(ref[...].astype(jnp.float32)) for ref in (own_ref, turned_ref, paired_ref, both_ref)]
    for place in range(4):
        step = jnp.bitwise_xor(at, place)
        value = held[3]
        for i in range(3):
            value = jnp.where(step == i, held[i], value)
        for i in range(out_ref.shape[0]):
            out_ref[i, place * rows : (place + 1) * rows, :] = value


def spread(pieces, after, count):
    rows, feature = pieces[0].shape
    return pl.pallas_call(
        spread_kernel,
        out_shape=jax.ShapeDtypeStruct((count, 4 * rows, feature), pieces[0].dtype),
        in_specs=[VMEM] * 4 + [ANY],
        out_specs=VMEM,
        compiler_params=params(4),
        cost_estimate=pl.CostEstimate(flops=0, bytes_accessed=count * rows * feature * 8, transcendentals=0),
        name="spread",
    )(*pieces, after)


def residual_rows(codes, codebook, store):
    tiles = codes.shape[1] // LANES
    table = codebook.astype(jnp.float32)
    low, high = table[:LANES].T, table[LANES:].T
    codes = codes.astype(jnp.float32).astype(jnp.bfloat16)
    stacked = jnp.concatenate(
        [codes[:, c * LANES : (c + 1) * LANES] for c in range(tiles)], axis=0
    )
    feature = lax.broadcasted_iota(jnp.int32, (LANES, LANES), 0)
    lane = lax.broadcasted_iota(jnp.int32, (LANES, LANES), 1)
    for jj in range(PER_TILE):
        pattern = (lane == jj * 32 + feature // 4).astype(jnp.float32).astype(jnp.bfloat16)
        index = lax.dot_general(pattern, stacked, NT, preferred_element_type=jnp.float32)
        index = index.astype(jnp.int32)
        within = index & (LANES - 1)
        parts = []
        for s in range(0, LANES, 8):
            w = within[s : s + 8]
            first = jnp.take_along_axis(low[s : s + 8], w, axis=1)
            second = jnp.take_along_axis(high[s : s + 8], w, axis=1)
            parts.append(jnp.where(index[s : s + 8] < LANES, first, second))
        store(jj, jnp.concatenate(parts, axis=0).T)


def residual_kernel(codes, book, lengths, out, live):
    def store(jj, rows):
        out[jj * LANES : (jj + 1) * LANES, :] = rows

    residual_rows(codes[...], book[...], store)
    count = live.shape[0]
    row = lax.broadcasted_iota(jnp.int32, (count, count), 0)
    lane = lax.broadcasted_iota(jnp.int32, (count, count), 1)
    held = jnp.where(row == lane, jnp.broadcast_to(lengths[...], (count, count)), 0)
    live[...] = jnp.broadcast_to(jnp.sum(held, axis=1, keepdims=True), live.shape)


def gather_kernel(ids, residual, table, out_ref):
    passages, slots = ids.shape
    tiles = slots // PER_TILE
    count = table.shape[0]
    span = passages * SLAB
    row = lax.broadcasted_iota(jnp.int32, (SLAB, LANES), 0).astype(jnp.int16)
    none = jnp.zeros((SLAB, LANES), jnp.bfloat16)
    fold = (
        lax.broadcasted_iota(jnp.int32, (passages, span), 0)
        == lax.broadcasted_iota(jnp.int32, (passages, span), 1) // SLAB
    ).astype(jnp.float32).astype(jnp.bfloat16)
    for m in range(slots):
        j = (m % tiles) * PER_TILE + m // tiles
        kept = []
        for p in range(passages):
            local = ids[p, j] & (count - 1)
            base = pl.multiple_of(local & ~(SLAB - 1), SLAB)
            wanted = jnp.full((SLAB, LANES), local & (SLAB - 1), jnp.int32).astype(jnp.int16)
            kept.append(jnp.where(row == wanted, table[pl.ds(base, SLAB), :], none))
        centre = jnp.dot(fold, jnp.concatenate(kept, axis=0), preferred_element_type=jnp.float32)
        at = m * passages
        out_ref[at : at + passages, :] = unit(centre + residual[at : at + passages, :])


def decode(slot_centroid, lengths, slot_codes, codebook, centroids):
    passages, slots = slot_centroid.shape
    rows, feature = passages * slots, codebook.shape[1]
    smem = pl.BlockSpec(memory_space=pltpu.SMEM)
    residual, live = pl.pallas_call(
        residual_kernel,
        out_shape=(
            jax.ShapeDtypeStruct((rows, feature), jnp.float32),
            jax.ShapeDtypeStruct((passages, LANES), jnp.int32),
        ),
        in_specs=[VMEM] * 3,
        out_specs=(VMEM, VMEM),
        compiler_params=params(4),
        cost_estimate=pl.CostEstimate(flops=rows * 256 * feature, bytes_accessed=rows * 256, transcendentals=0),
        name="residual",
    )(slot_codes, codebook, lengths.reshape(1, passages))
    vecs = pl.pallas_call(
        gather_kernel,
        out_shape=jax.ShapeDtypeStruct((rows, feature), jnp.bfloat16),
        in_specs=[smem, VMEM, VMEM],
        out_specs=VMEM,
        compiler_params=params(4 + centroids.size * 2 // (1 << 20)),
        cost_estimate=pl.CostEstimate(
            flops=rows * feature * 8, bytes_accessed=centroids.size * 2, transcendentals=rows
        ),
        name="gather",
    )(slot_centroid, residual, centroids)
    return vecs, live


def maxima(live, tokens, blocks, scratch, store):
    passages = live.shape[0]
    rows = scratch.shape[0] // len(blocks)
    slots = rows // passages
    tiles = slots // PER_TILE
    for b, (begin, vecs) in enumerate(blocks):
        first = vecs[0:passages, :]
        for m in range(slots):
            j = (m % tiles) * PER_TILE + m // tiles
            held = vecs[m * passages : (m + 1) * passages, :]
            if j:
                held = jnp.where(live > begin + j, held, first)
            at = b * rows + m * passages
            scratch[at : at + passages, :] = held

    chunk, span = 2048, 128
    for k in range(0, tokens.shape[0], chunk):
        wanted = tokens[k : k + chunk, :]
        best = None
        for b, (begin, _) in enumerate(blocks):
            top = None
            for s in range(b * rows, (b + 1) * rows, span):
                similar = lax.dot_general(
                    scratch[s : s + span, :], wanted, NT, preferred_element_type=jnp.float32
                )
                here = jnp.max(similar.reshape(span // passages, passages, chunk), axis=0)
                top = here if top is None else jnp.maximum(top, here)
            top = jnp.where(live[:, :1] > begin, top, LOWEST)
            best = top if best is None else jnp.maximum(best, top)
        store(k, best)


def begins(slots):
    own = lax.axis_index("grp")
    return [jnp.bitwise_xor(own, s) * slots for s in range(4)]


def first_kernel(live, tokens, own, other, far, best_out, scratch):
    begin = begins(own.shape[0] // live.shape[0])

    def store(k, best):
        best_out[:, k : k + best.shape[1]] = best

    blocks = list(zip(begin[:3], (own, other, far)))
    maxima(live[...], tokens, blocks, scratch, store)


def last_kernel(live, tokens, vecs, before, members, out_ref, scratch, whole):
    passages = live.shape[0]
    begin = begins(vecs.shape[0] // passages)

    def store(k, best):
        best = jnp.maximum(best, before[:, k : k + best.shape[1]])
        high = best.astype(jnp.bfloat16)
        rest = best - high.astype(jnp.float32)
        mid = rest.astype(jnp.bfloat16)
        low = (rest - mid.astype(jnp.float32)).astype(jnp.bfloat16)
        for i, part in enumerate((high, mid, low)):
            whole[i * passages : (i + 1) * passages, k : k + best.shape[1]] = part

    maxima(live[...], tokens, [(begin[3], vecs)], scratch, store)
    sums = lax.dot_general(members[...], whole[...], NT, preferred_element_type=jnp.float32)
    total = sums[:, 2 * passages : 3 * passages] + sums[:, passages : 2 * passages]
    total = total + sums[:, :passages]
    owners = out_ref.shape[0]
    for q in range(members.shape[0] // owners):
        out_ref[:, q * passages : (q + 1) * passages] = total[q * owners : (q + 1) * owners]


def params(mebibytes):
    return pltpu.CompilerParams(vmem_limit_bytes=mebibytes << 20)


def cost(tokens, rows, feature):
    return pl.CostEstimate(
        flops=2 * tokens * rows * feature,
        bytes_accessed=(tokens + rows) * feature * 2,
        transcendentals=tokens,
    )


def shards(queries, centroids, codebook, slot_codes, slot_centroid, lengths, candidates):
    own, query_len, feature = queries.shape
    owners = lax.axis_size("wide")
    passages = lengths.shape[0]
    tokens = owners * own * query_len
    rows = slot_centroid.size
    plain = queries.reshape(own * query_len, feature)
    members = members_of(own, owners, query_len)
    members, slot_codes = lax.optimization_barrier((members, slot_codes))
    pieces = [plain] + [
        lax.ppermute(plain, "wide", [(i, i ^ step) for i in range(owners)])
        for step in (TURN, PAIR, TURN ^ PAIR)
    ]
    vecs, live = decode(slot_centroid, lengths, slot_codes, codebook, centroids)
    sent = spread(pieces, vecs, owners // 4)
    base = [i for i in range(owners) if not i & (PAIR | UPPER)]
    groups = [[i ^ step for i in base] for step in (0, TURN, PAIR, TURN ^ PAIR)]
    gathered = lax.all_to_all(
        sent, "wide", split_axis=0, concat_axis=0, axis_index_groups=groups, tiled=True
    ).reshape(tokens, feature)

    core = [(i, i ^ 1) for i in range(4)]
    other = lax.ppermute(vecs, "grp", core)
    far = lax.ppermute(vecs, "grp", [(i, i ^ 2) for i in range(4)])
    far_other = lax.ppermute(far, "grp", core)
    best_shape = jax.ShapeDtypeStruct((passages, tokens), jnp.float32)
    block = pltpu.VMEM((rows, feature), jnp.bfloat16)
    best = pl.pallas_call(
        first_kernel,
        out_shape=best_shape,
        in_specs=[VMEM] * 5,
        out_specs=VMEM,
        scratch_shapes=[pltpu.VMEM((3 * rows, feature), jnp.bfloat16)],
        compiler_params=params(24),
        cost_estimate=cost(tokens, 3 * rows, feature),
        name="score_first",
    )(live, gathered, vecs, other, far)
    table = pl.pallas_call(
        last_kernel,
        out_shape=jax.ShapeDtypeStruct((owners, LANES), jnp.float32),
        in_specs=[VMEM] * 5,
        out_specs=VMEM,
        scratch_shapes=[block, pltpu.VMEM((3 * passages, tokens), jnp.bfloat16)],
        compiler_params=params(24),
        cost_estimate=cost(tokens, rows, feature),
        name="score_last",
    )(live, gathered, far_other, best, members)
    owned = lax.all_to_all(table, "wide", split_axis=0, concat_axis=0, tiled=True)
    return pick(owned, candidates, passages)


def pick_kernel(passages, owned_ref, candidates_ref, out_ref):
    owners = owned_ref.shape[0]
    count, wanted = candidates_ref.shape
    rows = lax.broadcasted_iota(jnp.int32, (owners, LANES), 0)
    held = owned_ref[...]
    for q in range(count):
        for c in range(0, wanted, LANES):
            ids = candidates_ref[q : q + 1, c : c + LANES]
            lane = jnp.broadcast_to(q * passages + ids % passages, (owners, LANES))
            part = jnp.broadcast_to(ids // passages, (owners, LANES))
            found = jnp.take_along_axis(held, lane, axis=1)
            out_ref[q : q + 1, c : c + LANES] = jnp.sum(
                jnp.where(rows == part, found, 0.0), axis=0, keepdims=True
            )


def pick(owned, candidates, passages):
    return pl.pallas_call(
        functools.partial(pick_kernel, passages),
        out_shape=jax.ShapeDtypeStruct(candidates.shape, jnp.float32),
        in_specs=[VMEM, VMEM],
        out_specs=VMEM,
        compiler_params=params(2),
        cost_estimate=pl.CostEstimate(
            flops=candidates.size * owned.shape[0] * 2, bytes_accessed=owned.size * 4, transcendentals=0
        ),
        name="pick",
    )(owned, candidates)


def solution(mesh):
    placed = (
        P(("grp", "wide"), None, None),
        P("grp", None),
        P(),
        P("wide", "grp"),
        P("wide", "grp"),
        P("wide"),
        P(("grp", "wide"), None),
    )
    return jax.shard_map(
        shards, mesh=mesh, in_specs=placed, out_specs=P(("grp", "wide"), None), check_vma=False
    )
```
